128 devices in a mesh: grp: 2 (over x_lo), ep: 64 (over x_hi, y, z, core).
Axes of the slice: x: 4 (x_hi: 2, x_lo: 2; x = x_hi * 2 + x_lo), y: 4, z: 4, core: 2. Of those that a mesh axis runs over, the one named last changes fastest.
Arguments:
- tokens: bfloat16 [16384, 2048], P(('grp', 'ep')), may hold values from -6 to 6
- cotangent: bfloat16 [16384, 2048], P(('grp', 'ep')), may hold values from -6 to 6
- combine: float32 [16384, 4], P(('grp', 'ep')), may hold values from 0.05 to 1
- route: int32 [16384, 4], P(('grp', 'ep')), may hold values from 0 to 127, all different within a row; in each aligned block of 128 rows (0 to 127, 128 to 255, ...) at most 6 rows name the same one
- anchors: int32 [64], replicated, may hold values from 0 to 63, as said below
- w_gate: bfloat16 [128, 2048, 768], P(('grp', 'ep')), may hold values from -0.125 to 0.125
- w_up: bfloat16 [128, 2048, 768], P(('grp', 'ep')), may hold values from -0.125 to 0.125
- w_down: bfloat16 [128, 768, 2048], P(('grp', 'ep')), may hold values from -0.21875 to 0.21875
Outputs:
- mixed: bfloat16 [16384, 2048], P(('grp', 'ep'))
- input_grad: bfloat16 [16384, 2048], P(('grp', 'ep'))
- grad_gate: float32 [64, 2048, 768], P('ep', 'grp')
- grad_up: float32 [64, 2048, 768], P('ep', 'grp')
- grad_down: float32 [64, 768, 2048], P('ep', None, 'grp')
The draws below stay inside these ranges and needn't reach their ends.
Inputs may be any that keep to these rules, and one draw needn't show every extreme that they name: route[t, k] names the slot g * 64 + p that choice k of token t goes to; a token's 4 choices name different slots; among the tokens of one device no slot is named more than 6 times. anchors[p] is p, or p - 1 for an odd p; every even p holds its own expert; anchors[63] = 62 and anchors[33] = 32.
All inputs are finite; a program needn't handle non-finite values.
Results may differ from the reference program's by a relative error of at most 0.0064.
Values may be sent and summed in bfloat16 or wider, within the bound.
No kernel may reach another device: no remote copies, remote signals or barrier semaphores. Data moves between devices by JAX's collectives and lax.ppermute only.
A program may use at most 192 MiB of HBM per device.

```python
import math
import jax
import jax.numpy as jnp
import numpy as np
from jax import lax

D = 2048
F = 768
TOP = 4
TOK_DEV = 128
SLOTS = 128
TOKENS = 16384
PAIR = 6
N_GRP = 2
N_EP = 64
DEVICES = 128


def draw_anchors(key, part):
    key = jax.random.fold_in(key, 7)
    pair_count = N_EP // 2
    pair_bits = jax.random.randint(key, (pair_count,), 0, 2)
    pair_ids = jnp.arange(pair_count)
    forced = (pair_ids == pair_count - 1) | (pair_ids == N_EP // 4)
    pair_bits = jnp.where(forced, 1, pair_bits).astype(jnp.int32)
    positions = jnp.arange(N_EP, dtype=jnp.int32)
    return (positions - positions % 2 * pair_bits[positions // 2]).astype(jnp.int32)


def levels(own_key, extent, pieces, least, top_value):
    def one(position, blocks):
        heights = jax.random.uniform(jax.random.fold_in(jax.random.fold_in(own_key, 6), position), (blocks,), jnp.float32, least / len(pieces), top_value / len(pieces))
        return jnp.repeat(jnp.exp(heights), extent[position] // blocks).reshape((-1,) + (1,) * (len(extent) - position - 1))

    gain = one(*pieces[0])
    for cut in pieces[1:]:
        gain = gain * one(*cut)
    return gain


def assign_block(key, own, number, rows, number_of, top, limit, lean):
    order = jax.random.permutation(key, number_of)
    crowded, common = portions_of(number_of, rows * top, limit, lean, True), portions_of(number_of, rows * top, limit, lean, False)
    places = jnp.arange(number_of)

    def named(tallies, offset_by):
        used = int((tallies > 0).sum())
        fixed = max(1, used // 4)
        shifted = fixed + (places - fixed + offset_by * (used - fixed)) % max(1, number_of - fixed)
        return jnp.zeros((number_of,), jnp.int32).at[order[jnp.where(places < fixed, places, shifted)]].set(jnp.asarray(tallies, jnp.int32))

    tallies = jnp.where(number % 4 == 0, named(crowded, number // 4), named(common, number - number // 4 - 1))
    mixed = jax.random.permutation(jax.random.fold_in(own, 3), number_of)
    donor, receiver = mixed[0:number_of // 2 * 2:2], mixed[1:number_of // 2 * 2:2]
    margin = jnp.minimum(tallies[donor] - 1, limit - tallies[receiver]) // 2
    margin = jnp.where((donor == order[0]) | (receiver == order[0]) | (tallies[receiver] == 0), 0, jnp.maximum(margin, 0))
    shifted = jax.random.randint(jax.random.fold_in(own, 4), (number_of // 2,), 0, 1 << 20) % (margin + 1)
    tallies = tallies.at[donor].add(-shifted).at[receiver].add(shifted)
    items = jnp.searchsorted(jnp.cumsum(tallies), jnp.arange(rows * top), side="right").astype(jnp.int32)
    grid = items.reshape(top, rows).T
    grid = grid[jax.random.permutation(jax.random.fold_in(own, 1), rows)]
    offset_by = jax.random.randint(jax.random.fold_in(own, 2), (rows, 1), 0, top)
    return jnp.take_along_axis(grid, (jnp.arange(top)[None, :] + offset_by) % top, axis=1)


def portions_of(amount, total, most, lean, full):
    weights = [(1 << 20) // math.isqrt(rank ** lean) + 1 for rank in range(1, amount + 1)]
    largest = most if full else min(most, max(-(-total // amount), total * weights[0] // sum(weights)))
    least = 1 if total - largest >= amount - 1 else 0
    holding, surplus = [largest] + [least] * (amount - 1), total - largest - least * (amount - 1)
    while surplus > 0:
        movable = [i for i in range(1, amount) if holding[i] < largest] or [i for i in range(1, amount) if holding[i] < most]
        whole, remaining = sum([weights[i] for i in movable]), surplus
        for i in movable:
            addition = min(most - holding[i], max(1, remaining * weights[i] // whole), surplus)
            holding[i] = holding[i] + addition
            surplus = surplus - addition
    return np.array(holding)


def centred(rng, dims, spread, limit, shards=(), kind=jnp.bfloat16):
    level = levels(rng, dims, shards, -0.22, 0.18) if shards else 1.0
    values = jax.random.normal(rng, dims, jnp.float32) * spread * level
    return jnp.minimum(jnp.maximum(values, -limit), limit).astype(kind)


def setup_inputs(seed: int = 0) -> dict:
    key_of = jax.random.split(jax.random.key(seed), 9)
    tokens = centred(key_of[0], (TOKENS, D), 1.0, 6.0, ((0, 128),))
    cotangent = centred(key_of[1], (TOKENS, D), 0.5, 6.0, ((0, 128),))
    combine = jnp.clip(jnp.exp(math.log(1.0) - 2.9957323 * jax.random.uniform(key_of[2], (TOKENS, TOP), jnp.float32) ** levels(key_of[2], (TOKENS, TOP), ((0, 128),), -0.2, 0.2)), 0.05, 1.0)
    route_keys = jax.random.split(jax.random.fold_in(key_of[3], 1), TOKENS // TOK_DEV)
    route_turns = jax.random.permutation(jax.random.fold_in(key_of[3], 3), TOKENS // TOK_DEV)
    route = jax.vmap(lambda own, number: assign_block(jax.random.fold_in(key_of[3], 2), own, number, TOK_DEV, DEVICES, TOP, PAIR, 2))(route_keys, route_turns).reshape((TOKENS, TOP))
    anchors = draw_anchors(jax.random.fold_in(key_of[8], 71), 0)
    w_gate = centred(key_of[5], (SLOTS, D, F), D ** -0.5, 0.125, ((0, 128),))
    w_up = centred(key_of[6], (SLOTS, D, F), D ** -0.5, 0.125, ((0, 128),))
    w_down = centred(key_of[7], (SLOTS, F, D), F ** -0.5, 0.21875, ((0, 128),))
    return dict(tokens=tokens, cotangent=cotangent, combine=combine, route=route, anchors=anchors, w_gate=w_gate, w_up=w_up, w_down=w_down)


def expert_pass(inputs, cot_rows, gate_weight, up_weight, down_weight):
    gate = jnp.dot(inputs, gate_weight, preferred_element_type=jnp.float32)
    up_proj = jnp.dot(inputs, up_weight, preferred_element_type=jnp.float32)
    sigma = jax.nn.sigmoid(gate)
    active = gate * sigma
    hidden = (active * up_proj).astype(jnp.bfloat16)
    expert_out = jnp.dot(hidden, down_weight, preferred_element_type=jnp.float32).astype(jnp.bfloat16)
    back = lax.dot_general(cot_rows, down_weight, (((1,), (1,)), ((), ())), preferred_element_type=jnp.float32)
    d_gate = (back * up_proj * sigma * (1.0 + gate * (1.0 - sigma))).astype(jnp.bfloat16)
    d_up = (back * active).astype(jnp.bfloat16)
    row_grad = (lax.dot_general(d_gate, gate_weight, (((1,), (1,)), ((), ())), preferred_element_type=jnp.float32)
                + lax.dot_general(d_up, up_weight, (((1,), (1,)), ((), ())), preferred_element_type=jnp.float32)).astype(jnp.bfloat16)
    part_gate = lax.dot_general(inputs, d_gate, (((0,), (0,)), ((), ())), preferred_element_type=jnp.float32).astype(jnp.bfloat16)
    part_up = lax.dot_general(inputs, d_up, (((0,), (0,)), ((), ())), preferred_element_type=jnp.float32).astype(jnp.bfloat16)
    part_down = lax.dot_general(hidden, cot_rows, (((0,), (0,)), ((), ())), preferred_element_type=jnp.float32).astype(jnp.bfloat16)
    return expert_out, row_grad, part_gate, part_up, part_down


def reference(tokens, cotangent, combine, route, anchors, w_gate, w_up, w_down):
    token_count = tokens.shape[0]
    width = tokens.shape[1]
    top_count = route.shape[1]
    slot_count = N_GRP * N_EP
    most_rows = slot_count * PAIR
    row_total = token_count * top_count
    holder = jnp.concatenate([jnp.arange(N_EP, dtype=jnp.int32), anchors.astype(jnp.int32)])
    flat = route.reshape(row_total).astype(jnp.int32)
    order = jnp.argsort(flat, stable=True).astype(jnp.int32)
    counts = jnp.zeros((slot_count,), jnp.int32).at[flat].add(1)
    starts = (jnp.cumsum(counts) - counts).astype(jnp.int32)
    padded_order = jnp.concatenate([order, jnp.full((most_rows,), row_total, jnp.int32)])
    tokens_ext = jnp.concatenate([tokens, jnp.zeros((1, width), tokens.dtype)])
    cot_ext = jnp.concatenate([cotangent, jnp.zeros((1, width), cotangent.dtype)])
    weight_ext = jnp.concatenate([combine.reshape(row_total), jnp.zeros((1,), combine.dtype)])

    def one_slot(carry, slot):
        outs_all, grads_all, sum_gate, sum_up, sum_down = carry
        picked = lax.dynamic_slice_in_dim(padded_order, starts[slot], most_rows)
        live = jnp.arange(most_rows, dtype=jnp.int32) < counts[slot]
        picked = jnp.where(live, picked, row_total).astype(jnp.int32)
        owner_token = (picked // top_count).astype(jnp.int32)
        inputs = tokens_ext[owner_token]
        cot_rows = (weight_ext[picked][:, None] * cot_ext[owner_token].astype(jnp.float32)).astype(jnp.bfloat16)
        expert = holder[slot]
        expert_out, row_grad, part_gate, part_up, part_down = expert_pass(
            inputs, cot_rows, w_gate[slot], w_up[slot], w_down[slot])
        outs_all = outs_all.at[picked].set(expert_out)
        grads_all = grads_all.at[picked].set(row_grad)
        sum_gate = sum_gate.at[expert].add(part_gate.astype(jnp.float32))
        sum_up = sum_up.at[expert].add(part_up.astype(jnp.float32))
        sum_down = sum_down.at[expert].add(part_down.astype(jnp.float32))
        return (outs_all, grads_all, sum_gate, sum_up, sum_down), None

    start_carry = (jnp.zeros((row_total + 1, width), jnp.bfloat16),
                   jnp.zeros((row_total + 1, width), jnp.bfloat16),
                   jnp.zeros((N_EP, w_gate.shape[1], w_gate.shape[2]), jnp.float32),
                   jnp.zeros((N_EP, w_up.shape[1], w_up.shape[2]), jnp.float32),
                   jnp.zeros((N_EP, w_down.shape[1], w_down.shape[2]), jnp.float32))
    final, _ = lax.scan(one_slot, start_carry, jnp.arange(slot_count, dtype=jnp.int32))
    outs_all, grads_all, grad_gate, grad_up, grad_down = final
    out_rows = outs_all[:row_total].reshape(token_count, top_count, width).astype(jnp.float32)
    mixed = jnp.sum(combine[:, :, None] * out_rows, axis=1).astype(jnp.bfloat16)
    grad_rows = grads_all[:row_total].reshape(token_count, top_count, width).astype(jnp.float32)
    input_grad = jnp.sum(grad_rows, axis=1).astype(jnp.bfloat16)
    return (mixed, input_grad, grad_gate, grad_up, grad_down)
```

```python
import functools

import jax
import jax.numpy as jnp
from jax import lax
from jax.experimental import pallas as pl
from jax.experimental.pallas import tpu as pltpu
from jax.sharding import Mesh, PartitionSpec as P

AXES = ("xlo", "xhi", "y", "z", "core")
PLANE = ("y", "z", "core")
LANES = 128
MIB = 1 << 20


def pack_kernel(pair_rows, dest, weight, tok_ref, cot_ref, out_ref, tok32, cot32):
    tokens, width = tok_ref.shape
    parts = width // LANES
    top = dest.shape[0] // tokens
    step = 1536
    blank = jnp.zeros((step, LANES), out_ref.dtype)

    @pl.loop(0, out_ref.shape[0] // step)
    def _(i):
        out_ref[pl.ds(pl.multiple_of(i * step, step), step), :] = blank

    for j in range(parts):
        cols = slice(j * LANES, (j + 1) * LANES)
        tok32[pl.ds(j, tokens, stride=parts), :] = tok_ref[:, cols].astype(jnp.float32)
        cot32[pl.ds(j, tokens, stride=parts), :] = cot_ref[:, cols].astype(jnp.float32)

    @pl.loop(0, tokens, unroll=2)
    def _(t):
        rows = pl.ds(pl.multiple_of(t * parts, parts), parts)
        tok = tok32[rows, :].astype(out_ref.dtype)
        cot = cot32[rows, :]
        for k in range(top):
            place = dest[t * top + k]
            out_ref[pl.ds(pl.multiple_of(place * parts, parts), parts), :] = tok
            out_ref[pl.ds(pl.multiple_of((place + pair_rows) * parts, parts), parts), :] = (
                cot * weight[t * top + k]
            ).astype(out_ref.dtype)


def pack(dest, weight, tokens, cotangent, slots, pair_rows):
    count, width = tokens.shape
    parts = width // LANES
    total = slots * 2 * pair_rows * parts
    return pl.pallas_call(
        functools.partial(pack_kernel, pair_rows),
        out_shape=jax.ShapeDtypeStruct((total, LANES), jnp.bfloat16),
        in_specs=[pl.BlockSpec(memory_space=pltpu.SMEM)] * 2
        + [pl.BlockSpec(memory_space=pltpu.VMEM)] * 2,
        out_specs=pl.BlockSpec(memory_space=pltpu.VMEM),
        scratch_shapes=[pltpu.VMEM((count * parts, LANES), jnp.float32)] * 2,
        compiler_params=pltpu.CompilerParams(vmem_limit_bytes=24 * MIB),
        cost_estimate=pl.CostEstimate(flops=0, bytes_accessed=12 * MIB, transcendentals=0),
    )(dest, weight, tokens, cotangent)


def unpack_kernel(in_ref, out_ref, wide):
    rings, members, _, tall, _ = in_ref.shape
    rows, width = out_ref.shape
    parts = width // LANES
    for m in range(members):
        for x in range(rings):
            wide[pl.ds((m * rings + x) * tall, tall), :] = in_ref[x, m, 0].astype(jnp.float32)
    for j in range(parts):
        out_ref[:, j * LANES : (j + 1) * LANES] = wide[pl.ds(j, rows, stride=parts), :].astype(
            out_ref.dtype
        )


def unpack(arrived, which, width):
    rings, plane, _, tall, _ = arrived.shape
    parts = width // LANES
    rows = rings * plane * tall // parts
    block = 8
    step = rows * block // plane
    return pl.pallas_call(
        unpack_kernel,
        grid=(plane // block,),
        out_shape=jax.ShapeDtypeStruct((rows, width), jnp.bfloat16),
        in_specs=[
            pl.BlockSpec((rings, block, 1, tall, LANES), lambda i: (0, i, which, 0, 0)),
        ],
        out_specs=pl.BlockSpec((step, width), lambda i: (i, 0)),
        scratch_shapes=[pltpu.VMEM((step * parts, LANES), jnp.float32)],
        compiler_params=pltpu.CompilerParams(vmem_limit_bytes=24 * MIB),
        cost_estimate=pl.CostEstimate(flops=0, bytes_accessed=6 * MIB, transcendentals=0),
    )(arrived)


def over(axes, sizes, move):
    pairs = []
    total = 1
    for n in sizes:
        total *= n
    for i in range(total):
        at, rest = [], i
        for n in reversed(sizes):
            at.append(rest % n)
            rest //= n
        to = move(tuple(reversed(at)))
        if to is not None:
            j = 0
            for n, c in zip(sizes, to, strict=True):
                j = j * n + c
            pairs.append((i, j))
    return pairs


def swap_low(block):
    return lax.ppermute(block, "xlo", [(0, 1), (1, 0)])


def swap_high(block):
    route = over(("xlo", "xhi"), (2, 2), lambda c: (1 - c[0], 1 - c[1]))
    return lax.ppermute(block, ("xlo", "xhi"), route)


def dot(a, b, over_a=1, over_b=0):
    return lax.dot_general(
        a, b, (((over_a,), (over_b,)), ((), ())), preferred_element_type=jnp.float32
    )


def on_device(tokens, cotangent, combine, route, anchors, w_gate, w_up, w_down):
    token_count, width = tokens.shape
    top = route.shape[1]
    rings = lax.axis_size(("xlo", "xhi"))
    plane = lax.axis_size(PLANE)
    slots = rings * plane
    row_count = token_count * top
    pair_rows = 3 * row_count // (2 * slots)
    parts = width // LANES
    half = width // 2
    group = lax.axis_index("xlo")
    ring_at = lax.axis_index(("xlo", "xhi"))
    ep_index = lax.axis_index(("xhi",) + PLANE)
    ep_count = lax.axis_size(("xhi",) + PLANE)

    target = route.reshape(row_count)
    marks = (target[:, None] == jnp.arange(slots, dtype=jnp.int32)[None, :]).astype(jnp.int32)
    rank = jnp.sum(jnp.cumsum(marks, axis=0) * marks, axis=1) - 1
    packed = pack(
        target * (2 * pair_rows) + rank, combine.reshape(row_count), tokens, cotangent, slots, pair_rows
    )
    arrived = lax.all_to_all(
        packed.reshape(slots, 2 * pair_rows * parts, LANES), AXES, 0, 0, tiled=True
    ).reshape(rings, plane, 2, pair_rows * parts, LANES)

    ring_of = jnp.full((token_count, 1), ring_at, jnp.float32)
    facts = jnp.concatenate(
        [target.reshape(token_count, top).astype(jnp.float32), rank.reshape(token_count, top).astype(jnp.float32), combine, ring_of],
        axis=1,
    )
    near = jnp.concatenate([facts, swap_low(facts)])
    facts = jnp.concatenate([swap_high(near), near])
    slot_of = facts[:, :top].astype(jnp.int32) - ring_at * plane
    rank_of = facts[:, top : 2 * top].astype(jnp.int32)
    weight_of = facts[:, 2 * top : 3 * top]
    ring_of = facts[:, 3 * top :].astype(jnp.int32)
    inside = (slot_of >= 0) & (slot_of < plane)
    column = jnp.where(inside, (slot_of * rings + ring_of) * pair_rows + rank_of, -1)
    places = jnp.arange(slots * pair_rows, dtype=jnp.int32)[None, :]
    coarse_of = lax.reduce_precision(weight_of, 8, 7)
    fine_of = weight_of - coarse_of
    ones, coarse, fine = 0.0, 0.0, 0.0
    for k in range(top):
        hit = column[:, k : k + 1] == places
        ones = ones + jnp.where(hit, 1.0, 0.0)
        coarse = coarse + jnp.where(hit, coarse_of[:, k : k + 1], 0.0)
        fine = fine + jnp.where(hit, fine_of[:, k : k + 1], 0.0)
    ones = ones.astype(jnp.bfloat16)
    coarse = coarse.astype(jnp.bfloat16)
    fine = fine.astype(jnp.bfloat16)

    gate_weight, up_weight, down_weight = w_gate[0], w_up[0], w_down[0]
    inputs = unpack(arrived, 0, width)
    gate = dot(inputs, gate_weight)
    up_proj = dot(inputs, up_weight)
    sigma = jax.nn.sigmoid(gate)
    active = gate * sigma
    hidden = (active * up_proj).astype(jnp.bfloat16)
    expert_out = dot(hidden, down_weight).astype(jnp.bfloat16)
    cot_in = unpack(arrived, 1, width)
    back = dot(cot_in, down_weight, 1, 1)
    d_gate = (back * up_proj * sigma * (1.0 + gate * (1.0 - sigma))).astype(jnp.bfloat16)
    d_up = (back * active).astype(jnp.bfloat16)

    def to_plane(rows):
        chunks = rows.reshape(plane, rings * pair_rows, width)
        return lax.all_to_all(chunks, PLANE, 0, 0, tiled=True).reshape(slots * pair_rows, width)

    def home(sums):
        far = swap_high(sums(slice(0, 2 * token_count)).astype(jnp.bfloat16)).astype(jnp.float32)
        mine = sums(slice(2 * token_count, 3 * token_count)) + far[:token_count]
        others = sums(slice(3 * token_count, 4 * token_count)) + far[token_count:]
        return (mine + swap_low(others.astype(jnp.bfloat16)).astype(jnp.float32)).astype(jnp.bfloat16)

    out_rows = to_plane(expert_out)

    def halves_of(array, which):
        return lax.dynamic_slice_in_dim(array, which * half, half, 1)

    away_in, away_cot = halves_of(inputs, 1 - group), halves_of(cot_in, 1 - group)
    here_in, here_cot = halves_of(inputs, group), halves_of(cot_in, group)
    send = [
        dot(hidden, away_cot, 0, 0).astype(jnp.bfloat16),
        dot(away_in, d_gate, 0, 0).astype(jnp.bfloat16),
        dot(away_in, d_up, 0, 0).astype(jnp.bfloat16),
    ]
    received = [swap_low(s) for s in send]
    row_grad = (dot(d_gate, gate_weight, 1, 1) + dot(d_up, up_weight, 1, 1)).astype(jnp.bfloat16)
    grad_rows = to_plane(row_grad)
    kept = [
        dot(hidden, here_cot, 0, 0).astype(jnp.bfloat16),
        dot(here_in, d_gate, 0, 0).astype(jnp.bfloat16),
        dot(here_in, d_up, 0, 0).astype(jnp.bfloat16),
    ]
    is_anchor = anchors[ep_index] == ep_index
    beside = jnp.minimum(ep_index + 1, ep_count - 1)
    joins = (ep_index + 1 < ep_count) & (anchors[beside] == ep_index)
    totals = []
    for keep, got in zip(kept, received, strict=True):
        passed = lax.ppermute(jnp.where(group == 0, got, keep), "core", [(1, 0)]).astype(jnp.float32)
        keep, got = keep.astype(jnp.float32), got.astype(jnp.float32)
        first = jnp.where(group == 0, keep, got)
        second = jnp.where(group == 0, got, keep)
        totals.append(first + jnp.where(is_anchor, second, 0.0) + jnp.where(joins, passed, 0.0))

    mixed = home(lambda s: dot(coarse[s], out_rows) + dot(fine[s], out_rows))
    input_grad = home(lambda s: dot(ones[s], grad_rows))
    grad_down, grad_gate, grad_up = totals
    return (mixed, input_grad, grad_gate[None], grad_up[None], grad_down[None])


def solution(mesh):
    fine = Mesh(mesh.devices.reshape(2, 2, 4, 4, 2), AXES)
    rows = P(AXES, None)
    slot = P(AXES, None, None)
    experts = ("xhi",) + PLANE
    return jax.shard_map(
        on_device,
        mesh=fine,
        in_specs=(rows, rows, rows, rows, P(), slot, slot, slot),
        out_specs=(
            rows,
            rows,
            P(experts, "xlo", None),
            P(experts, "xlo", None),
            P(experts, None, "xlo"),
        ),
        check_vma=False,
    )
```

```python
import functools

import jax
import jax.numpy as jnp
from jax import lax
from jax.experimental import pallas as pl
from jax.experimental.pallas import tpu as pltpu
from jax.sharding import Mesh, PartitionSpec as P

AXES = ("xlo", "xhi", "y", "z", "core")
PLANE = ("y", "z", "core")
LANES = 128
MIB = 1 << 20


def pack_kernel(pair_rows, route_ref, weight_ref, tok_ref, cot_ref, out_ref, rank_ref, place):
    top, tokens = route_ref.shape
    targets, _, tall, _ = out_ref.shape
    slots = targets * pl.num_programs(0)
    rows = targets * pair_rows
    parts = tall // pair_rows
    step = pl.program_id(0)

    @pl.when(step == 0)
    def _():
        across = lax.broadcasted_iota(jnp.int32, (tokens, tokens), 1)
        down = lax.broadcasted_iota(jnp.int32, (tokens, tokens), 0)
        earlier = (down < across).astype(jnp.bfloat16)
        slot = lax.broadcasted_iota(jnp.int32, (slots, tokens), 0)
        before = jnp.zeros((slots, 1), jnp.float32)
        for k in range(top):
            mine = slot == route_ref[k : k + 1, :]
            marks = mine.astype(jnp.float32)
            ahead = jnp.dot(
                marks.astype(jnp.bfloat16), earlier, preferred_element_type=jnp.float32
            )
            rank = jnp.sum(jnp.where(mine, ahead + before, 0.0), axis=0, keepdims=True)
            before = before + jnp.sum(marks, axis=1, keepdims=True)
            rank_ref[k : k + 1, :] = rank.astype(jnp.int32)
            place[k : k + 1, :] = route_ref[k : k + 1, :] * pair_rows + rank.astype(jnp.int32)

    row = lax.broadcasted_iota(jnp.int32, (rows, tokens), 0) + step * rows
    chosen = jnp.zeros((rows, tokens), jnp.float32)
    weight = jnp.zeros((rows, tokens), jnp.float32)
    for k in range(top):
        hit = row == place[k : k + 1, :]
        chosen = jnp.where(hit, 1.0, chosen)
        weight = jnp.where(hit, weight_ref[k : k + 1, :], weight)
    weight = jnp.sum(weight, axis=1, keepdims=True)
    chosen = chosen.astype(jnp.bfloat16)
    tok = jnp.dot(chosen, tok_ref[...], preferred_element_type=jnp.float32)
    out_ref[:, 0] = tok.reshape(targets, tall, LANES).astype(out_ref.dtype)
    cot = jnp.dot(chosen, cot_ref[...], preferred_element_type=jnp.float32) * weight
    out_ref[:, 1] = cot.reshape(targets, tall, LANES).astype(out_ref.dtype)


def pack(route, weight, tokens, cotangent, slots, pair_rows):
    count, width = tokens.shape
    tall = pair_rows * width // LANES
    block = 16
    whole = lambda i: (0, 0)
    return pl.pallas_call(
        functools.partial(pack_kernel, pair_rows),
        grid=(slots // block,),
        out_shape=(
            pltpu.HBM((slots, 2, tall, LANES), jnp.bfloat16),
            jax.ShapeDtypeStruct(route.shape, jnp.int32),
        ),
        in_specs=[
            pl.BlockSpec(route.shape, whole),
            pl.BlockSpec(weight.shape, whole),
            pl.BlockSpec(tokens.shape, whole),
            pl.BlockSpec(cotangent.shape, whole),
        ],
        out_specs=(
            pl.BlockSpec((block, 2, tall, LANES), lambda i: (i, 0, 0, 0)),
            pl.BlockSpec(route.shape, whole),
        ),
        scratch_shapes=[pltpu.VMEM(route.shape, jnp.int32)],
        compiler_params=pltpu.CompilerParams(vmem_limit_bytes=24 * MIB),
        cost_estimate=cheap(),
    )(route, weight, tokens, cotangent)


def unpack_kernel(in_ref, tok_ref, cot_ref):
    rings, members, _, tall, _ = in_ref.shape
    rows, width = tok_ref.shape
    parts = width // LANES
    for which, out_ref in enumerate((tok_ref, cot_ref)):
        value = in_ref[:, :, which].astype(jnp.float32)
        value = value.reshape(rings, members, tall // parts, parts, LANES)
        out_ref[...] = jnp.swapaxes(value, 0, 1).reshape(rows, width).astype(out_ref.dtype)


def unpack(arrived, width):
    rings, plane, _, tall, _ = arrived.shape
    rows = rings * plane * tall * LANES // width
    block = 8
    step = rows * block // plane
    return pl.pallas_call(
        unpack_kernel,
        grid=(plane // block,),
        out_shape=(jax.ShapeDtypeStruct((rows, width), jnp.bfloat16),) * 2,
        in_specs=[
            pl.BlockSpec((rings, block, 2, tall, LANES), lambda i: (0, i, 0, 0, 0)),
        ],
        out_specs=(pl.BlockSpec((step, width), lambda i: (i, 0)),) * 2,
        compiler_params=pltpu.CompilerParams(vmem_limit_bytes=24 * MIB),
        cost_estimate=cheap(),
    )(arrived)


def dot(a, b, over_a=1, over_b=0):
    return lax.dot_general(
        a, b, (((over_a,), (over_b,)), ((), ())), preferred_element_type=jnp.float32
    )


def cheap(flops=0):
    return pl.CostEstimate(flops=flops, bytes_accessed=0, transcendentals=0)


def fixed(shape, at=(0, 0)):
    return pl.BlockSpec(shape, lambda n, g: at, pipeline_mode=pl.Buffered(1))


def away(shape):
    return pl.BlockSpec(shape, lambda n, g: (0, 1 - g[0]), pipeline_mode=pl.Buffered(1))


def here(shape):
    return pl.BlockSpec(shape, lambda n, g: (0, g[0]), pipeline_mode=pl.Buffered(1))


def down(shape):
    return pl.BlockSpec(shape, lambda n, g: (n, 0))


def across(shape):
    return pl.BlockSpec(shape, lambda n, g: (0, n))


def call(kernel, group, steps, ins, outs, *operands):
    return pl.pallas_call(
        kernel,
        grid_spec=pltpu.PrefetchScalarGridSpec(
            num_scalar_prefetch=1,
            grid=(steps,),
            in_specs=ins,
            out_specs=tuple(spec for spec, _, _ in outs),
        ),
        out_shape=tuple(pltpu.HBM(shape, kind) for _, shape, kind in outs),
        compiler_params=pltpu.CompilerParams(vmem_limit_bytes=40 * MIB),
        cost_estimate=cheap(),
    )(group, *operands)


def first_kernel(group, x_ref, c_ref, gate_w, up_w, gate_ref, up_ref, hidden_ref, send_ref):
    gate = dot(x_ref[...], gate_w[...])
    up = dot(x_ref[...], up_w[...])
    gate_ref[...] = gate
    up_ref[...] = up
    hidden = (gate * jax.nn.sigmoid(gate) * up).astype(jnp.bfloat16)
    hidden_ref[...] = hidden
    send_ref[...] = dot(hidden, c_ref[...], 0, 0).astype(jnp.bfloat16)


def first(group, inputs, cot_in, gate_w, up_w):
    rows, width = inputs.shape
    inner = gate_w.shape[1]
    block, half = 256, width // 2
    f32, b16 = jnp.float32, jnp.bfloat16
    return call(
        first_kernel,
        group,
        inner // block,
        [fixed((rows, width)), away((rows, half)), across((width, block)), across((width, block))],
        [
            (across((rows, block)), (rows, inner), f32),
            (across((rows, block)), (rows, inner), f32),
            (across((rows, block)), (rows, inner), b16),
            (down((block, half)), (inner, half), b16),
        ],
        inputs,
        cot_in,
        gate_w,
        up_w,
    )


def expert_kernel(group, hidden_ref, down_w, out_ref):
    out_ref[...] = dot(hidden_ref[...], down_w[...]).astype(jnp.bfloat16)


def expert(group, hidden, down_w):
    rows, inner = hidden.shape
    width, block = down_w.shape[1], 512
    return call(
        expert_kernel,
        group,
        width // block,
        [fixed((rows, inner)), across((inner, block))],
        [(across((rows, block)), (rows, width), jnp.bfloat16)],
        hidden,
        down_w,
    )[0]


def second_kernel(group, x_ref, c_ref, down_w, gate_ref, up_ref, dg_ref, du_ref, send_g, send_u):
    back = dot(c_ref[...], down_w[...], 1, 1)
    gate, up = gate_ref[...], up_ref[...]
    sigma = jax.nn.sigmoid(gate)
    d_gate = (back * up * sigma * (1.0 + gate * (1.0 - sigma))).astype(jnp.bfloat16)
    d_up = (back * (gate * sigma)).astype(jnp.bfloat16)
    dg_ref[...] = d_gate
    du_ref[...] = d_up
    send_g[...] = dot(x_ref[...], d_gate, 0, 0).astype(jnp.bfloat16)
    send_u[...] = dot(x_ref[...], d_up, 0, 0).astype(jnp.bfloat16)


def second(group, inputs, cot_in, down_w, gate, up):
    rows, width = inputs.shape
    inner = gate.shape[1]
    block, half = 256, width // 2
    b16 = jnp.bfloat16
    return call(
        second_kernel,
        group,
        inner // block,
        [
            away((rows, half)),
            fixed((rows, width)),
            down((block, width)),
            across((rows, block)),
            across((rows, block)),
        ],
        [
            (across((rows, block)), (rows, inner), b16),
            (across((rows, block)), (rows, inner), b16),
            (across((half, block)), (half, inner), b16),
            (across((half, block)), (half, inner), b16),
        ],
        inputs,
        cot_in,
        down_w,
        gate,
        up,
    )


def rows_kernel(group, dg_ref, du_ref, gate_w, up_w, out_ref):
    out_ref[...] = (dot(dg_ref[...], gate_w[...], 1, 1) + dot(du_ref[...], up_w[...], 1, 1)).astype(
        jnp.bfloat16
    )


def row_gradient(group, d_gate, d_up, gate_w, up_w):
    rows, inner = d_gate.shape
    width, block = gate_w.shape[0], 512
    return call(
        rows_kernel,
        group,
        width // block,
        [fixed((rows, inner)), fixed((rows, inner)), down((block, inner)), down((block, inner))],
        [(across((rows, block)), (rows, width), jnp.bfloat16)],
        d_gate,
        d_up,
        gate_w,
        up_w,
    )[0]


def keep_kernel(group, x_ref, c_ref, hidden_ref, dg_ref, du_ref, keep_d, keep_g, keep_u):
    keep_d[...] = dot(hidden_ref[...], c_ref[...], 0, 0).astype(jnp.bfloat16)
    keep_g[...] = dot(x_ref[...], dg_ref[...], 0, 0).astype(jnp.bfloat16)
    keep_u[...] = dot(x_ref[...], du_ref[...], 0, 0).astype(jnp.bfloat16)


def keep_half(group, inputs, cot_in, hidden, d_gate, d_up):
    rows, width = inputs.shape
    inner = hidden.shape[1]
    block, half = 256, width // 2
    b16 = jnp.bfloat16
    return call(
        keep_kernel,
        group,
        inner // block,
        [here((rows, half)), here((rows, half))] + [across((rows, block))] * 3,
        [
            (down((block, half)), (inner, half), b16),
            (across((half, block)), (half, inner), b16),
            (across((half, block)), (half, inner), b16),
        ],
        inputs,
        cot_in,
        hidden,
        d_gate,
        d_up,
    )


def sums_kernel(group, *refs):
    *weights, rows_ref, far_ref, near_ref = refs
    total = sum(dot(w[...], rows_ref[...], 0, 0) for w in weights)
    count = far_ref.shape[0]
    far_ref[...] = total[:count].astype(jnp.bfloat16)
    near_ref[...] = total[count:]


def sums(group, rows, *weights):
    count, targets = weights[0].shape
    width, block = rows.shape[1], 512
    part = targets // 2
    return call(
        sums_kernel,
        group,
        width // block,
        [fixed((count, targets)) for _ in weights] + [across((count, block))],
        [
            (across((part, block)), (part, width), jnp.bfloat16),
            (across((part, block)), (part, width), jnp.float32),
        ],
        *weights,
        rows,
    )


def over(axes, sizes, move):
    pairs = []
    total = 1
    for n in sizes:
        total *= n
    for i in range(total):
        at, rest = [], i
        for n in reversed(sizes):
            at.append(rest % n)
            rest //= n
        to = move(tuple(reversed(at)))
        if to is not None:
            j = 0
            for n, c in zip(sizes, to, strict=True):
                j = j * n + c
            pairs.append((i, j))
    return pairs


def swap_low(block):
    return lax.ppermute(block, "xlo", [(0, 1), (1, 0)])


def swap_high(block):
    route = over(("xlo", "xhi"), (2, 2), lambda c: (1 - c[0], 1 - c[1]))
    return lax.ppermute(block, ("xlo", "xhi"), route)


def after(value, *others):
    return lax.optimization_barrier((value,) + others)[0]


def on_device(tokens, cotangent, combine, route, anchors, w_gate, w_up, w_down):
    token_count, width = tokens.shape
    top = route.shape[1]
    rings = lax.axis_size(("xlo", "xhi"))
    plane = lax.axis_size(PLANE)
    slots = rings * plane
    pair_rows = 3 * token_count * top // (2 * slots)
    half = width // 2
    group = lax.axis_index("xlo")
    high = lax.axis_index("xhi")
    ring_at = lax.axis_index(("xlo", "xhi"))
    ep_index = lax.axis_index(("xhi",) + PLANE)
    ep_count = lax.axis_size(("xhi",) + PLANE)

    weight = jnp.transpose(combine)
    target = jnp.transpose(route)
    packed, rank = pack(target, weight, tokens, cotangent, slots, pair_rows)
    arrived = lax.all_to_all(packed.reshape(slots, -1, LANES), AXES, 0, 0, tiled=True).reshape(
        rings, plane, 2, -1, LANES
    )

    facts = jnp.concatenate([target.astype(jnp.float32), rank.astype(jnp.float32), weight, weight])
    def weights_of(facts):
        near = jnp.concatenate([facts, swap_low(facts)])
        facts = jnp.concatenate([swap_high(near), near]).reshape(rings, 4, top, token_count)
        ring_of = jnp.stack(
            [
                (1 - group) * 2 + 1 - high,
                group * 2 + 1 - high,
                group * 2 + high,
                (1 - group) * 2 + high,
            ]
        )[:, None, None]
        slot_of = facts[:, 0].astype(jnp.int32) - ring_at * plane
        rank_of = facts[:, 1].astype(jnp.int32)
        inside = (slot_of >= 0) & (slot_of < plane)
        column = jnp.where(inside, (slot_of * rings + ring_of) * pair_rows + rank_of, -1)
        places = jnp.arange(slots * pair_rows, dtype=jnp.int32)[:, None, None]
        coarse_of = lax.reduce_precision(facts[:, 2], 8, 7)
        fine_of = facts[:, 2] - coarse_of
        ones, coarse, fine = 0.0, 0.0, 0.0
        for k in range(top):
            hit = column[None, :, k] == places
            ones = ones + jnp.where(hit, 1.0, 0.0)
            coarse = coarse + jnp.where(hit, coarse_of[None, :, k], 0.0)
            fine = fine + jnp.where(hit, fine_of[None, :, k], 0.0)
        return [
            w.astype(jnp.bfloat16).reshape(slots * pair_rows, rings * token_count)
            for w in (coarse, fine, ones)
        ]

    def to_plane(rows):
        chunks = rows.reshape(plane, rings * pair_rows, width)
        return lax.all_to_all(chunks, PLANE, 0, 0, tiled=True).reshape(slots * pair_rows, width)

    gate_weight, up_weight, down_weight = w_gate[0], w_up[0], w_down[0]
    at = group.astype(jnp.int32).reshape(1)
    inputs, cot_in = unpack(arrived, width)
    gate, up_proj, hidden, send_down = first(at, inputs, cot_in, gate_weight, up_weight)
    got_down = swap_low(send_down)
    expert_out = expert(at, hidden, down_weight)
    out_rows = to_plane(expert_out)
    d_gate, d_up, send_gate, send_up = second(
        at, inputs, after(cot_in, expert_out), down_weight, gate, up_proj
    )
    got_gate, got_up = swap_low(send_gate), swap_low(send_up)
    row_grad = row_gradient(at, d_gate, d_up, gate_weight, up_weight)
    grad_rows = to_plane(after(row_grad, got_down))
    kept = keep_half(at, inputs, cot_in, after(hidden, row_grad), d_gate, d_up)
    coarse, fine, ones = weights_of(after(facts, send_up))
    out_rows = after(out_rows, coarse, fine, ones)

    is_anchor = anchors[ep_index] == ep_index
    beside = jnp.minimum(ep_index + 1, ep_count - 1)
    joins = (ep_index + 1 < ep_count) & (anchors[beside] == ep_index)

    def joined(keep, got):
        passed = lax.ppermute(jnp.where(group == 0, got, keep), "core", [(1, 0)]).astype(jnp.float32)
        keep, got = keep.astype(jnp.float32), got.astype(jnp.float32)
        one = jnp.where(group == 0, keep, got)
        two = jnp.where(group == 0, got, keep)
        return one + jnp.where(is_anchor, two, 0.0) + jnp.where(joins, passed, 0.0)

    out_far, out_near = sums(at, out_rows, coarse, fine)
    out_came = swap_high(out_far)
    got_down = after(got_down, out_far)
    grad_down = joined(kept[0], got_down)
    out_near = after(out_near, got_gate) + out_came.astype(jnp.float32)
    out_others = out_near[token_count:].astype(jnp.bfloat16)
    out_last = swap_low(out_others)
    grad_gate = joined(kept[1], got_gate)
    row_far, row_near = sums(at, after(grad_rows, out_others, got_up), ones)
    row_came = swap_high(row_far)
    got_up = after(got_up, row_far)
    grad_up = joined(kept[2], got_up)
    out_last = after(out_last, row_far)
    mixed = (out_near[:token_count] + out_last.astype(jnp.float32)).astype(jnp.bfloat16)
    row_near = row_near + row_came.astype(jnp.float32)
    row_others = row_near[token_count:].astype(jnp.bfloat16)
    row_last = swap_low(row_others).astype(jnp.float32)
    input_grad = (row_near[:token_count] + row_last).astype(jnp.bfloat16)
    return (mixed, input_grad, grad_gate[None], grad_up[None], grad_down[None])


def solution(mesh):
    fine = Mesh(mesh.devices.reshape(2, 2, 4, 4, 2), AXES)
    rows = P(AXES, None)
    slot = P(AXES, None, None)
    experts = ("xhi",) + PLANE
    return jax.shard_map(
        on_device,
        mesh=fine,
        in_specs=(rows, rows, rows, rows, P(), slot, slot, slot),
        out_specs=(
            rows,
            rows,
            P(experts, "xlo", None),
            P(experts, "xlo", None),
            P(experts, None, "xlo"),
        ),
        check_vma=False,
    )
```

```python
import functools

import jax
import jax.numpy as jnp
from jax import lax
from jax.experimental import pallas as pl
from jax.experimental.pallas import tpu as pltpu
from jax.sharding import Mesh, PartitionSpec as P

AXES = ("xlo", "xhi", "y", "z", "core")
PLANE = ("y", "z", "core")
LANES = 128
MIB = 1 << 20


def pack_kernel(pair_rows, route_ref, weight_ref, tok_ref, cot_ref, out_ref, rank_ref, place):
    top, tokens = route_ref.shape
    targets, _, tall, _ = out_ref.shape
    slots = targets * pl.num_programs(0)
    rows = targets * pair_rows
    parts = tall // pair_rows
    step = pl.program_id(0)

    @pl.when(step == 0)
    def _():
        across = lax.broadcasted_iota(jnp.int32, (tokens, tokens), 1)
        down = lax.broadcasted_iota(jnp.int32, (tokens, tokens), 0)
        earlier = (down < across).astype(jnp.bfloat16)
        slot = lax.broadcasted_iota(jnp.int32, (slots, tokens), 0)
        before = jnp.zeros((slots, 1), jnp.float32)
        for k in range(top):
            mine = slot == route_ref[k : k + 1, :]
            marks = mine.astype(jnp.float32)
            ahead = jnp.dot(
                marks.astype(jnp.bfloat16), earlier, preferred_element_type=jnp.float32
            )
            rank = jnp.sum(jnp.where(mine, ahead + before, 0.0), axis=0, keepdims=True)
            before = before + jnp.sum(marks, axis=1, keepdims=True)
            rank_ref[k : k + 1, :] = rank.astype(jnp.int32)
            place[k : k + 1, :] = route_ref[k : k + 1, :] * pair_rows + rank.astype(jnp.int32)

    row = lax.broadcasted_iota(jnp.int32, (rows, tokens), 0) + step * rows
    chosen = jnp.zeros((rows, tokens), jnp.float32)
    weight = jnp.zeros((rows, tokens), jnp.float32)
    for k in range(top):
        hit = row == place[k : k + 1, :]
        chosen = jnp.where(hit, 1.0, chosen)
        weight = jnp.where(hit, weight_ref[k : k + 1, :], weight)
    weight = jnp.sum(weight, axis=1, keepdims=True)
    chosen = chosen.astype(jnp.bfloat16)
    tok = jnp.dot(chosen, tok_ref[...], preferred_element_type=jnp.float32)
    out_ref[:, 0] = tok.reshape(targets, tall, LANES).astype(out_ref.dtype)
    cot = jnp.dot(chosen, cot_ref[...], preferred_element_type=jnp.float32) * weight
    out_ref[:, 1] = cot.reshape(targets, tall, LANES).astype(out_ref.dtype)


def pack(route, weight, tokens, cotangent, slots, pair_rows):
    count, width = tokens.shape
    tall = pair_rows * width // LANES
    block = 16
    whole = lambda i: (0, 0)
    return pl.pallas_call(
        functools.partial(pack_kernel, pair_rows),
        grid=(slots // block,),
        out_shape=(
            pltpu.HBM((slots, 2, tall, LANES), jnp.bfloat16),
            jax.ShapeDtypeStruct(route.shape, jnp.int32),
        ),
        in_specs=[
            pl.BlockSpec(route.shape, whole),
            pl.BlockSpec(weight.shape, whole),
            pl.BlockSpec(tokens.shape, whole),
            pl.BlockSpec(cotangent.shape, whole),
        ],
        out_specs=(
            pl.BlockSpec((block, 2, tall, LANES), lambda i: (i, 0, 0, 0)),
            pl.BlockSpec(route.shape, whole),
        ),
        scratch_shapes=[pltpu.VMEM(route.shape, jnp.int32)],
        compiler_params=pltpu.CompilerParams(vmem_limit_bytes=60 * MIB),
        cost_estimate=cheap(),
    )(route, weight, tokens, cotangent)


def dot(a, b, over_a=1, over_b=0):
    return lax.dot_general(
        a, b, (((over_a,), (over_b,)), ((), ())), preferred_element_type=jnp.float32
    )


def cheap(flops=0):
    return pl.CostEstimate(flops=flops, bytes_accessed=0, transcendentals=0)


def fixed(shape, at=(0, 0)):
    return pl.BlockSpec(shape, lambda n, g: at, pipeline_mode=pl.Buffered(1))


def down(shape):
    return pl.BlockSpec(shape, lambda n, g: (n, 0))


def across(shape):
    return pl.BlockSpec(shape, lambda n, g: (0, n))


def call(kernel, group, steps, ins, outs, *operands, scratch=(), vmem=56 * MIB):
    return pl.pallas_call(
        kernel,
        grid_spec=pltpu.PrefetchScalarGridSpec(
            num_scalar_prefetch=1,
            grid=(steps,),
            in_specs=ins,
            out_specs=tuple(spec for spec, _, _ in outs),
            scratch_shapes=list(scratch),
        ),
        out_shape=tuple(pltpu.HBM(shape, kind) for _, shape, kind in outs),
        compiler_params=pltpu.CompilerParams(vmem_limit_bytes=vmem),
        cost_estimate=cheap(),
    )(group, *operands)


def front_kernel(
    group,
    arrived,
    gate_in,
    up_in,
    down_in,
    x_out,
    c_out,
    gate_out,
    up_out,
    hidden_out,
    down_out,
    expert_out,
    landed,
    gate_w,
    up_w,
    down_w,
    x_all,
    c_all,
    gate_all,
    up_all,
    hidden,
    send_down,
    expert_all,
    in_sems,
    w_sems,
    out_sems,
):
    rings, plane, _, tall, _ = arrived.shape
    steps, _, members = landed.shape[:3]
    _, rows, half = x_all.shape
    width = 2 * half
    parts = width // LANES
    inner = hidden.shape[1]
    block, wide = 256, 512
    some = rows // steps
    mine = 1 - group[0]
    fetches = [
        pltpu.make_async_copy(
            arrived.at[:, pl.ds(i * members, members)], landed.at[i], in_sems.at[i]
        )
        for i in range(steps)
    ]
    loads = [
        pltpu.make_async_copy(source, target, w_sems.at[i])
        for i, (source, target) in enumerate(
            ((gate_in, gate_w), (up_in, up_w), (down_in, down_w))
        )
    ]
    for copy in fetches + loads:
        copy.start()
    sent = []

    def put(source, target):
        copy = pltpu.make_async_copy(source, target, out_sems.at[len(sent)])
        copy.start()
        sent.append(copy)

    for i in range(steps):
        fetches[i].wait()
        for which, out in enumerate((x_all, c_all)):
            value = landed[i, :, :, which].astype(jnp.float32)
            value = value.reshape(rings, members, tall // parts, parts, LANES)
            value = jnp.swapaxes(value, 0, 1).reshape(some, width).astype(jnp.bfloat16)
            out[0, i * some : (i + 1) * some, :] = value[:, :half]
            out[1, i * some : (i + 1) * some, :] = value[:, half:]
    loads[0].wait()
    loads[1].wait()
    for n in range(inner // block):
        cols = slice(n * block, (n + 1) * block)
        gate = dot(x_all[0], gate_w[:half, cols]) + dot(x_all[1], gate_w[half:, cols])
        up = dot(x_all[0], up_w[:half, cols]) + dot(x_all[1], up_w[half:, cols])
        gate_all[:, cols] = gate
        up_all[:, cols] = up
        hidden[:, cols] = (gate * jax.nn.sigmoid(gate) * up).astype(jnp.bfloat16)
        send_down[cols, :] = dot(hidden[:, cols], c_all[mine], 0, 0).astype(jnp.bfloat16)
    put(send_down, down_out)
    loads[2].wait()
    for n in range(width // wide):
        cols = slice(n * wide, (n + 1) * wide)
        expert_all[:, cols] = dot(hidden[...], down_w[:, cols]).astype(jnp.bfloat16)
    put(expert_all, expert_out)
    put(x_all, x_out)
    put(c_all, c_out)
    put(gate_all, gate_out)
    put(up_all, up_out)
    put(hidden, hidden_out)
    for copy in sent:
        copy.wait()


def front(group, arrived, gate_w, up_w, down_w):
    rings, plane, _, tall, _ = arrived.shape
    width, inner = gate_w.shape
    rows = rings * plane * tall * LANES // width
    half, members = width // 2, 8
    steps = plane // members
    f32, b16 = jnp.float32, jnp.bfloat16
    shapes = [
        ((2, rows, half), b16),
        ((2, rows, half), b16),
        ((rows, inner), f32),
        ((rows, inner), f32),
        ((rows, inner), b16),
        ((inner, half), b16),
        ((rows, width), b16),
    ]
    weights = [((width, inner), b16), ((width, inner), b16), ((inner, width), b16)]
    return pl.pallas_call(
        front_kernel,
        out_shape=tuple(pltpu.HBM(*shape) for shape in shapes),
        in_specs=[pl.BlockSpec(memory_space=pltpu.SMEM)]
        + [pl.BlockSpec(memory_space=pl.ANY)] * 4,
        out_specs=tuple(pl.BlockSpec(memory_space=pl.ANY) for _ in shapes),
        scratch_shapes=[pltpu.VMEM((steps, rings, members, 2, tall, LANES), b16)]
        + [pltpu.VMEM(*shape) for shape in weights + shapes]
        + [pltpu.SemaphoreType.DMA((n,)) for n in (steps, len(weights), len(shapes))],
        compiler_params=pltpu.CompilerParams(vmem_limit_bytes=56 * MIB),
        cost_estimate=cheap(),
    )(group, arrived, gate_w, up_w, down_w)


def second_kernel(group, x_ref, c_ref, down_w, gate_ref, up_ref, dg_ref, du_ref, send_ref, turned):
    @pl.when(pl.program_id(0) == 0)
    def _():
        turned[...] = jnp.transpose(x_ref[0])

    half = x_ref.shape[2]
    back = dot(c_ref[0], down_w[:, :half], 1, 1) + dot(c_ref[1], down_w[:, half:], 1, 1)
    gate, up = gate_ref[...], up_ref[...]
    sigma = jax.nn.sigmoid(gate)
    d_gate = (back * up * sigma * (1.0 + gate * (1.0 - sigma))).astype(jnp.bfloat16)
    d_up = (back * (gate * sigma)).astype(jnp.bfloat16)
    dg_ref[...] = d_gate
    du_ref[...] = d_up
    send_ref[0] = dot(turned[...], d_gate).astype(jnp.bfloat16)
    send_ref[1] = dot(turned[...], d_up).astype(jnp.bfloat16)


def second(group, inputs, cot_in, down_w, gate, up):
    _, rows, half = inputs.shape
    inner = gate.shape[1]
    block, width = 256, 2 * half
    b16 = jnp.bfloat16
    away = pl.BlockSpec((1, rows, half), lambda n, g: (1 - g[0], 0, 0), pipeline_mode=pl.Buffered(1))
    return call(
        second_kernel,
        group,
        inner // block,
        [
            away,
            fixed((2, rows, half), (0, 0, 0)),
            down((block, width)),
            across((rows, block)),
            across((rows, block)),
        ],
        [
            (across((rows, block)), (rows, inner), b16),
            (across((rows, block)), (rows, inner), b16),
            (pl.BlockSpec((2, half, block), lambda n, g: (0, 0, n)), (2, half, inner), b16),
        ],
        inputs,
        cot_in,
        down_w,
        gate,
        up,
        scratch=[pltpu.VMEM((half, rows), b16)],
    )


def rows_kernel(group, dg_ref, du_ref, gate_w, up_w, out_ref):
    out_ref[...] = (dot(dg_ref[...], gate_w[...], 1, 1) + dot(du_ref[...], up_w[...], 1, 1)).astype(
        jnp.bfloat16
    )


def row_gradient(group, which, d_gate, d_up, gate_w, up_w):
    rows, inner = d_gate.shape
    width, block = gate_w.shape[0] // 2, 512
    steps = width // block
    part = pl.BlockSpec((block, inner), lambda n, g: (n + which * steps, 0))
    return call(
        rows_kernel,
        group,
        steps,
        [fixed((rows, inner)), fixed((rows, inner)), part, part],
        [(across((rows, block)), (rows, width), jnp.bfloat16)],
        d_gate,
        d_up,
        gate_w,
        up_w,
    )[0]


def keep_kernel(group, x_ref, c_ref, hidden_ref, dg_ref, du_ref, keep_d, keep_g, keep_u):
    keep_d[...] = dot(hidden_ref[...], c_ref[0], 0, 0).astype(jnp.bfloat16)
    turned = jnp.transpose(x_ref[0])
    keep_g[...] = dot(turned, dg_ref[...]).astype(jnp.bfloat16)
    keep_u[...] = dot(turned, du_ref[...]).astype(jnp.bfloat16)


def keep_half(group, inputs, cot_in, hidden, d_gate, d_up):
    _, rows, half = inputs.shape
    inner = hidden.shape[1]
    block = 384
    b16 = jnp.bfloat16
    here = pl.BlockSpec((1, rows, half), lambda n, g: (g[0], 0, 0), pipeline_mode=pl.Buffered(1))
    return call(
        keep_kernel,
        group,
        inner // block,
        [here, here] + [across((rows, block))] * 3,
        [
            (down((block, half)), (inner, half), b16),
            (across((half, block)), (half, inner), b16),
            (across((half, block)), (half, inner), b16),
        ],
        inputs,
        cot_in,
        hidden,
        d_gate,
        d_up,
    )


def sums_kernel(group, *refs):
    *weights, rows_ref, far_ref, near_ref = refs
    total = sum(dot(w[...], rows_ref[...], 0, 0) for w in weights)
    count = far_ref.shape[0]
    far_ref[...] = total[:count].astype(jnp.bfloat16)
    near_ref[...] = total[count:]


def sums(group, rows, *weights):
    count, targets = weights[0].shape
    width, block = rows.shape[1], 512
    part = targets // 2
    return call(
        sums_kernel,
        group,
        width // block,
        [fixed((count, targets)) for _ in weights] + [across((count, block))],
        [
            (across((part, block)), (part, width), jnp.bfloat16),
            (across((part, block)), (part, width), jnp.float32),
        ],
        *weights,
        rows,
    )


def over(axes, sizes, move):
    pairs = []
    total = 1
    for n in sizes:
        total *= n
    for i in range(total):
        at, rest = [], i
        for n in reversed(sizes):
            at.append(rest % n)
            rest //= n
        to = move(tuple(reversed(at)))
        if to is not None:
            j = 0
            for n, c in zip(sizes, to, strict=True):
                j = j * n + c
            pairs.append((i, j))
    return pairs


def swap_low(block):
    return lax.ppermute(block, "xlo", [(0, 1), (1, 0)])


def swap_high(block):
    route = over(("xlo", "xhi"), (2, 2), lambda c: (1 - c[0], 1 - c[1]))
    return lax.ppermute(block, ("xlo", "xhi"), route)


def after(value, *others):
    return lax.optimization_barrier((value,) + others)[0]


def on_device(tokens, cotangent, combine, route, anchors, w_gate, w_up, w_down):
    token_count, width = tokens.shape
    top = route.shape[1]
    rings = lax.axis_size(("xlo", "xhi"))
    plane = lax.axis_size(PLANE)
    slots = rings * plane
    pair_rows = 3 * token_count * top // (2 * slots)
    half = width // 2
    group = lax.axis_index("xlo")
    high = lax.axis_index("xhi")
    ring_at = lax.axis_index(("xlo", "xhi"))
    ep_index = lax.axis_index(("xhi",) + PLANE)
    ep_count = lax.axis_size(("xhi",) + PLANE)

    weight = jnp.transpose(combine)
    target = jnp.transpose(route)
    packed, rank = pack(target, weight, tokens, cotangent, slots, pair_rows)
    arrived = lax.all_to_all(packed.reshape(slots, -1, LANES), AXES, 0, 0, tiled=True).reshape(
        rings, plane, 2, -1, LANES
    )

    facts = jnp.concatenate([target.astype(jnp.float32), rank.astype(jnp.float32), weight, weight])
    opposite = lax.ppermute(facts, "xhi", [(0, 1), (1, 0)])
    facts = [swap_high(facts), opposite, facts, swap_low(facts)]
    arrived, *facts = lax.optimization_barrier((arrived, *facts))

    def weights_of(facts):
        facts = jnp.stack(facts).reshape(rings, 4, top, token_count)
        ring_of = jnp.stack(
            [
                (1 - group) * 2 + 1 - high,
                group * 2 + 1 - high,
                group * 2 + high,
                (1 - group) * 2 + high,
            ]
        )[:, None, None]
        slot_of = facts[:, 0].astype(jnp.int32) - ring_at * plane
        rank_of = facts[:, 1].astype(jnp.int32)
        inside = (slot_of >= 0) & (slot_of < plane)
        column = jnp.where(inside, (slot_of * rings + ring_of) * pair_rows + rank_of, -1)
        places = jnp.arange(slots * pair_rows, dtype=jnp.int32)[:, None, None]
        coarse_of = lax.reduce_precision(facts[:, 2], 8, 7)
        fine_of = facts[:, 2] - coarse_of
        ones, coarse, fine = 0.0, 0.0, 0.0
        for k in range(top):
            hit = column[None, :, k] == places
            ones = ones + jnp.where(hit, 1.0, 0.0)
            coarse = coarse + jnp.where(hit, coarse_of[None, :, k], 0.0)
            fine = fine + jnp.where(hit, fine_of[None, :, k], 0.0)
        return [
            w.astype(jnp.bfloat16).reshape(slots * pair_rows, rings * token_count)
            for w in (coarse, fine, ones)
        ]

    def to_plane(rows):
        chunks = rows.reshape(plane, rings * pair_rows, -1)
        return lax.all_to_all(chunks, PLANE, 0, 0, tiled=True).reshape(slots * pair_rows, -1)

    gate_weight, up_weight, down_weight = w_gate[0], w_up[0], w_down[0]
    at = group.astype(jnp.int32).reshape(1)
    inputs, cot_in, gate, up_proj, hidden, send_down, expert_out = front(
        at, arrived, gate_weight, up_weight, down_weight
    )
    got_down = swap_low(send_down)
    out_rows = to_plane(expert_out)
    d_gate, d_up, send_both = second(at, inputs, cot_in, down_weight, gate, up_proj)
    got_both = swap_low(send_both)
    row_left = row_gradient(at, 0, d_gate, d_up, gate_weight, up_weight)
    left_rows = to_plane(after(row_left, got_down))
    row_right = row_gradient(at, 1, after(d_gate, row_left), d_up, gate_weight, up_weight)
    right_rows = to_plane(row_right)
    coarse, fine, ones = weights_of(lax.optimization_barrier((*facts, row_right))[:-1])
    out_rows = after(out_rows, coarse, fine, ones)
    out_far, out_near = sums(at, out_rows, coarse, fine)
    kept = keep_half(at, inputs, cot_in, after(hidden, out_far), d_gate, d_up)

    is_anchor = anchors[ep_index] == ep_index
    beside = jnp.minimum(ep_index + 1, ep_count - 1)
    joins = (ep_index + 1 < ep_count) & (anchors[beside] == ep_index)

    def joined(keep, got):
        passed = lax.ppermute(jnp.where(group == 0, got, keep), "core", [(1, 0)]).astype(jnp.float32)
        keep, got = keep.astype(jnp.float32), got.astype(jnp.float32)
        one = jnp.where(group == 0, keep, got)
        two = jnp.where(group == 0, got, keep)
        return one + jnp.where(is_anchor, two, 0.0) + jnp.where(joins, passed, 0.0)

    grad_down = joined(kept[0], after(got_down, out_far))
    out_came = swap_high(out_far)
    out_near = out_near + out_came.astype(jnp.float32)
    out_others = out_near[token_count:].astype(jnp.bfloat16)
    out_last = swap_low(out_others)
    left_far, left_near = sums(at, after(left_rows, out_others), ones)
    left_came = swap_high(left_far)
    right_far, right_near = sums(at, after(right_rows, left_far, got_both), ones)
    right_came = swap_high(right_far)
    got_both = after(got_both, right_far)
    grad_gate = joined(kept[1], got_both[0])
    grad_up = joined(kept[2], got_both[1])
    out_last = after(out_last, right_far)
    mixed = (out_near[:token_count] + out_last.astype(jnp.float32)).astype(jnp.bfloat16)
    ends = []
    for near, came in ((left_near, left_came), (right_near, right_came)):
        near = near + came.astype(jnp.float32)
        last = swap_low(near[token_count:].astype(jnp.bfloat16)).astype(jnp.float32)
        ends.append((near[:token_count] + last).astype(jnp.bfloat16))
    input_grad = jnp.concatenate(ends, axis=1)
    return (mixed, input_grad, grad_gate[None], grad_up[None], grad_down[None])


def solution(mesh):
    fine = Mesh(mesh.devices.reshape(2, 2, 4, 4, 2), AXES)
    rows = P(AXES, None)
    slot = P(AXES, None, None)
    experts = ("xhi",) + PLANE
    return jax.shard_map(
        on_device,
        mesh=fine,
        in_specs=(rows, rows, rows, rows, P(), slot, slot, slot),
        out_specs=(
            rows,
            rows,
            P(experts, "xlo", None),
            P(experts, "xlo", None),
            P(experts, None, "xlo"),
        ),
        check_vma=False,
    )
```

```python
import functools

import jax
import jax.numpy as jnp
from jax import lax
from jax.experimental import pallas as pl
from jax.experimental.pallas import tpu as pltpu
from jax.sharding import Mesh, PartitionSpec as P

AXES = ("xlo", "xhi", "y", "z", "core")
PLANE = ("y", "z", "core")
LANES = 128
MIB = 1 << 20
LONG = 40_000_000_000


def pack_kernel(pair_rows, route_ref, weight_ref, tok_ref, cot_ref, out_ref, rank_ref, place):
    top, tokens = route_ref.shape
    targets, _, tall, _ = out_ref.shape
    slots = targets * pl.num_programs(0)
    rows = targets * pair_rows
    parts = tall // pair_rows
    step = pl.program_id(0)

    @pl.when(step == 0)
    def _():
        across = lax.broadcasted_iota(jnp.int32, (tokens, tokens), 1)
        down = lax.broadcasted_iota(jnp.int32, (tokens, tokens), 0)
        earlier = (down < across).astype(jnp.bfloat16)
        slot = lax.broadcasted_iota(jnp.int32, (slots, tokens), 0)
        before = jnp.zeros((slots, 1), jnp.float32)
        for k in range(top):
            mine = slot == route_ref[k : k + 1, :]
            marks = mine.astype(jnp.float32)
            ahead = jnp.dot(
                marks.astype(jnp.bfloat16), earlier, preferred_element_type=jnp.float32
            )
            rank = jnp.sum(jnp.where(mine, ahead + before, 0.0), axis=0, keepdims=True)
            before = before + jnp.sum(marks, axis=1, keepdims=True)
            rank_ref[k : k + 1, :] = rank.astype(jnp.int32)
            place[k : k + 1, :] = route_ref[k : k + 1, :] * pair_rows + rank.astype(jnp.int32)

    row = lax.broadcasted_iota(jnp.int32, (rows, tokens), 0) + step * rows
    chosen = jnp.zeros((rows, tokens), jnp.float32)
    weight = jnp.zeros((rows, tokens), jnp.float32)
    for k in range(top):
        hit = row == place[k : k + 1, :]
        chosen = jnp.where(hit, 1.0, chosen)
        weight = jnp.where(hit, weight_ref[k : k + 1, :], weight)
    weight = jnp.sum(weight, axis=1, keepdims=True)
    chosen = chosen.astype(jnp.bfloat16)
    tok = jnp.dot(chosen, tok_ref[...], preferred_element_type=jnp.float32)
    out_ref[:, 0] = tok.reshape(targets, tall, LANES).astype(out_ref.dtype)
    cot = jnp.dot(chosen, cot_ref[...], preferred_element_type=jnp.float32) * weight
    out_ref[:, 1] = cot.reshape(targets, tall, LANES).astype(out_ref.dtype)


def pack(route, weight, tokens, cotangent, slots, pair_rows):
    count, width = tokens.shape
    tall = pair_rows * width // LANES
    block = 16
    whole = lambda i: (0, 0)
    return pl.pallas_call(
        functools.partial(pack_kernel, pair_rows),
        grid=(slots // block,),
        out_shape=(
            pltpu.HBM((slots, 2, tall, LANES), jnp.bfloat16),
            jax.ShapeDtypeStruct(route.shape, jnp.int32),
        ),
        in_specs=[
            pl.BlockSpec(route.shape, whole),
            pl.BlockSpec(weight.shape, whole),
            pl.BlockSpec(tokens.shape, whole),
            pl.BlockSpec(cotangent.shape, whole),
        ],
        out_specs=(
            pl.BlockSpec((block, 2, tall, LANES), lambda i: (i, 0, 0, 0)),
            pl.BlockSpec(route.shape, whole),
        ),
        scratch_shapes=[pltpu.VMEM(route.shape, jnp.int32)],
        compiler_params=pltpu.CompilerParams(vmem_limit_bytes=60 * MIB),
        cost_estimate=cheap(),
    )(route, weight, tokens, cotangent)


def dot(a, b, over_a=1, over_b=0):
    return lax.dot_general(
        a, b, (((over_a,), (over_b,)), ((), ())), preferred_element_type=jnp.float32
    )


def cheap(flops=0):
    return pl.CostEstimate(flops=flops, bytes_accessed=0, transcendentals=0)


def fixed(shape, at=(0, 0)):
    return pl.BlockSpec(shape, lambda n, g: at, pipeline_mode=pl.Buffered(1))


def down(shape):
    return pl.BlockSpec(shape, lambda n, g: (n, 0))


def across(shape):
    return pl.BlockSpec(shape, lambda n, g: (0, n))


def call(kernel, group, steps, ins, outs, *operands, scratch=(), vmem=56 * MIB, cost=0):
    return pl.pallas_call(
        kernel,
        grid_spec=pltpu.PrefetchScalarGridSpec(
            num_scalar_prefetch=1,
            grid=(steps,),
            in_specs=ins,
            out_specs=tuple(spec for spec, _, _ in outs),
            scratch_shapes=list(scratch),
        ),
        out_shape=tuple(pltpu.HBM(shape, kind) for _, shape, kind in outs),
        compiler_params=pltpu.CompilerParams(vmem_limit_bytes=vmem),
        cost_estimate=cheap(cost),
    )(group, *operands)


def front_kernel(
    group,
    arrived,
    gate_in,
    up_in,
    x_out,
    c_out,
    gate_out,
    up_out,
    hidden_out,
    down_out,
    landed,
    gate_w,
    up_w,
    x_all,
    c_all,
    gate_all,
    up_all,
    hidden,
    send_down,
    in_sems,
    w_sems,
    out_sems,
):
    rings, plane, _, tall, _ = arrived.shape
    steps, _, members = landed.shape[:3]
    _, rows, half = x_all.shape
    width = 2 * half
    parts = width // LANES
    inner = hidden.shape[1]
    block = gate_all.shape[2]
    some = rows // steps
    mine = 1 - group[0]
    fetches = [
        pltpu.make_async_copy(
            arrived.at[:, pl.ds(i * members, members)], landed.at[i], in_sems.at[i]
        )
        for i in range(steps)
    ]
    loads = [
        pltpu.make_async_copy(source, target, w_sems.at[i])
        for i, (source, target) in enumerate(
            ((gate_in, gate_w), (up_in, up_w))
        )
    ]
    for copy in fetches + loads:
        copy.start()
    sent = []

    def put(source, target):
        copy = pltpu.make_async_copy(source, target, out_sems.at[len(sent)])
        copy.start()
        sent.append(copy)

    for i in range(steps):
        fetches[i].wait()
        for which, out in enumerate((x_all, c_all)):
            value = landed[i, :, :, which].astype(jnp.float32)
            value = value.reshape(rings, members, tall // parts, parts, LANES)
            value = jnp.swapaxes(value, 0, 1).reshape(some, width).astype(jnp.bfloat16)
            out[0, i * some : (i + 1) * some, :] = value[:, :half]
            out[1, i * some : (i + 1) * some, :] = value[:, half:]
    for copy in loads:
        copy.wait()
    put(x_all, x_out)
    put(c_all, c_out)
    for n in range(inner // block):
        cols = slice(n * block, (n + 1) * block)
        gate = dot(x_all[0], gate_w[:half, cols]) + dot(x_all[1], gate_w[half:, cols])
        up = dot(x_all[0], up_w[:half, cols]) + dot(x_all[1], up_w[half:, cols])
        gate_all[n] = gate
        up_all[n] = up
        put(gate_all.at[n], gate_out.at[n])
        put(up_all.at[n], up_out.at[n])
        hidden[:, cols] = (gate * jax.nn.sigmoid(gate) * up).astype(jnp.bfloat16)
        send_down[cols, :] = dot(hidden[:, cols], c_all[mine], 0, 0).astype(jnp.bfloat16)
        put(send_down.at[cols], down_out.at[cols])
    put(hidden, hidden_out)
    for copy in sent:
        copy.wait()


def front(group, arrived, gate_w, up_w):
    rings, plane, _, tall, _ = arrived.shape
    width, inner = gate_w.shape
    rows = rings * plane * tall * LANES // width
    half, members, block = width // 2, 8, 256
    steps = plane // members
    f32, b16 = jnp.float32, jnp.bfloat16
    shapes = [
        ((2, rows, half), b16),
        ((2, rows, half), b16),
        ((inner // block, rows, block), f32),
        ((inner // block, rows, block), f32),
        ((rows, inner), b16),
        ((inner, half), b16),
    ]
    weights = [((width, inner), b16)] * 2
    sends = 3 + 3 * (inner // block)
    return pl.pallas_call(
        front_kernel,
        out_shape=tuple(pltpu.HBM(*shape) for shape in shapes),
        in_specs=[pl.BlockSpec(memory_space=pltpu.SMEM)]
        + [pl.BlockSpec(memory_space=pl.ANY)] * 3,
        out_specs=tuple(pl.BlockSpec(memory_space=pl.ANY) for _ in shapes),
        scratch_shapes=[pltpu.VMEM((steps, rings, members, 2, tall, LANES), b16)]
        + [pltpu.VMEM(*shape) for shape in weights + shapes]
        + [pltpu.SemaphoreType.DMA((n,)) for n in (steps, len(weights), sends)],
        compiler_params=pltpu.CompilerParams(vmem_limit_bytes=56 * MIB),
        cost_estimate=cheap(),
    )(group, arrived, gate_w, up_w)


def expert_kernel(group, hidden_ref, down_w, out_ref):
    out_ref[...] = dot(hidden_ref[...], down_w[...]).astype(jnp.bfloat16)


def expert(group, hidden, down_w):
    rows, inner = hidden.shape
    width, block = down_w.shape[1], 512
    return call(
        expert_kernel,
        group,
        width // block,
        [fixed((rows, inner)), across((inner, block))],
        [(across((rows, block)), (rows, width), jnp.bfloat16)],
        hidden,
        down_w,
    )[0]


def second_kernel(group, x_ref, c_ref, down_w, gate_ref, up_ref, dg_ref, du_ref, send_ref, turned):
    @pl.when(pl.program_id(0) == 0)
    def _():
        turned[...] = jnp.transpose(x_ref[0])

    half = x_ref.shape[2]
    back = dot(c_ref[0], down_w[:, :half], 1, 1) + dot(c_ref[1], down_w[:, half:], 1, 1)
    gate, up = gate_ref[0], up_ref[0]
    sigma = jax.nn.sigmoid(gate)
    d_gate = (back * up * sigma * (1.0 + gate * (1.0 - sigma))).astype(jnp.bfloat16)
    d_up = (back * (gate * sigma)).astype(jnp.bfloat16)
    dg_ref[...] = d_gate
    du_ref[...] = d_up
    send_ref[0] = dot(turned[...], d_gate).astype(jnp.bfloat16)
    send_ref[1] = dot(turned[...], d_up).astype(jnp.bfloat16)


def second(group, inputs, cot_in, down_w, gate, up):
    _, rows, half = inputs.shape
    chunks, _, block = gate.shape
    inner, width = chunks * block, 2 * half
    chunk = pl.BlockSpec((1, rows, block), lambda n, g: (n, 0, 0))
    b16 = jnp.bfloat16
    away = pl.BlockSpec((1, rows, half), lambda n, g: (1 - g[0], 0, 0), pipeline_mode=pl.Buffered(1))
    return call(
        second_kernel,
        group,
        inner // block,
        [
            away,
            fixed((2, rows, half), (0, 0, 0)),
            down((block, width)),
            chunk,
            chunk,
        ],
        [
            (across((rows, block)), (rows, inner), b16),
            (across((rows, block)), (rows, inner), b16),
            (pl.BlockSpec((2, half, block), lambda n, g: (0, 0, n)), (2, half, inner), b16),
        ],
        inputs,
        cot_in,
        down_w,
        gate,
        up,
        scratch=[pltpu.VMEM((half, rows), b16)],
    )


def rows_kernel(group, dg_ref, du_ref, gate_w, up_w, out_ref):
    out_ref[...] = (dot(dg_ref[...], gate_w[...], 1, 1) + dot(du_ref[...], up_w[...], 1, 1)).astype(
        jnp.bfloat16
    )


def row_gradient(group, first, steps, block, cost, d_gate, d_up, gate_w, up_w):
    rows, inner = d_gate.shape
    part = pl.BlockSpec((block, inner), lambda n, g: (n + first, 0))
    return call(
        rows_kernel,
        group,
        steps,
        [fixed((rows, inner)), fixed((rows, inner)), part, part],
        [(across((rows, block)), (rows, steps * block), jnp.bfloat16)],
        d_gate,
        d_up,
        gate_w,
        up_w,
        cost=cost,
    )[0]


def keep_kernel(group, x_ref, c_ref, hidden_ref, dg_ref, du_ref, keep_d, keep_g, keep_u):
    keep_d[...] = dot(hidden_ref[...], c_ref[0], 0, 0).astype(jnp.bfloat16)
    turned = jnp.transpose(x_ref[0])
    keep_g[...] = dot(turned, dg_ref[...]).astype(jnp.bfloat16)
    keep_u[...] = dot(turned, du_ref[...]).astype(jnp.bfloat16)


def keep_half(group, inputs, cot_in, hidden, d_gate, d_up):
    _, rows, half = inputs.shape
    inner = hidden.shape[1]
    block = 384
    b16 = jnp.bfloat16
    here = pl.BlockSpec((1, rows, half), lambda n, g: (g[0], 0, 0), pipeline_mode=pl.Buffered(1))
    return call(
        keep_kernel,
        group,
        inner // block,
        [here, here] + [across((rows, block))] * 3,
        [
            (down((block, half)), (inner, half), b16),
            (across((half, block)), (half, inner), b16),
            (across((half, block)), (half, inner), b16),
        ],
        inputs,
        cot_in,
        hidden,
        d_gate,
        d_up,
    )


def sums_kernel(group, *refs):
    *weights, rows_ref, far_ref, near_ref = refs
    total = sum(dot(w[...], rows_ref[...], 0, 0) for w in weights)
    count = far_ref.shape[0]
    far_ref[...] = total[:count].astype(jnp.bfloat16)
    near_ref[...] = total[count:]


def sums(group, rows, *weights):
    count, targets = weights[0].shape
    width, block = rows.shape[1], 256
    part = targets // 2
    return call(
        sums_kernel,
        group,
        width // block,
        [fixed((count, targets)) for _ in weights] + [across((count, block))],
        [
            (across((part, block)), (part, width), jnp.bfloat16),
            (across((part, block)), (part, width), jnp.float32),
        ],
        *weights,
        rows,
    )


def over(axes, sizes, move):
    pairs = []
    total = 1
    for n in sizes:
        total *= n
    for i in range(total):
        at, rest = [], i
        for n in reversed(sizes):
            at.append(rest % n)
            rest //= n
        to = move(tuple(reversed(at)))
        if to is not None:
            j = 0
            for n, c in zip(sizes, to, strict=True):
                j = j * n + c
            pairs.append((i, j))
    return pairs


def swap_low(block):
    return lax.ppermute(block, "xlo", [(0, 1), (1, 0)])


def swap_high(block):
    route = over(("xlo", "xhi"), (2, 2), lambda c: (1 - c[0], 1 - c[1]))
    return lax.ppermute(block, ("xlo", "xhi"), route)


def after(value, *others):
    return lax.optimization_barrier((value,) + others)[0]


def on_device(tokens, cotangent, combine, route, anchors, w_gate, w_up, w_down):
    token_count, width = tokens.shape
    top = route.shape[1]
    rings = lax.axis_size(("xlo", "xhi"))
    plane = lax.axis_size(PLANE)
    slots = rings * plane
    pair_rows = 3 * token_count * top // (2 * slots)
    half = width // 2
    group = lax.axis_index("xlo")
    high = lax.axis_index("xhi")
    ring_at = lax.axis_index(("xlo", "xhi"))
    ep_index = lax.axis_index(("xhi",) + PLANE)
    ep_count = lax.axis_size(("xhi",) + PLANE)

    weight = jnp.transpose(combine)
    target = jnp.transpose(route)
    packed, rank = pack(target, weight, tokens, cotangent, slots, pair_rows)
    arrived = lax.all_to_all(packed.reshape(slots, -1, LANES), AXES, 0, 0, tiled=True).reshape(
        rings, plane, 2, -1, LANES
    )

    facts = jnp.concatenate([target.astype(jnp.float32), rank.astype(jnp.float32), weight, weight])
    opposite = lax.ppermute(facts, "xhi", [(0, 1), (1, 0)])
    facts = [swap_high(facts), opposite, facts, swap_low(facts)]
    arrived, *facts = lax.optimization_barrier((arrived, *facts))

    def weights_of(facts):
        facts = jnp.stack(facts).reshape(rings, 4, top, token_count)
        ring_of = jnp.stack(
            [
                (1 - group) * 2 + 1 - high,
                group * 2 + 1 - high,
                group * 2 + high,
                (1 - group) * 2 + high,
            ]
        )[:, None, None]
        slot_of = facts[:, 0].astype(jnp.int32) - ring_at * plane
        rank_of = facts[:, 1].astype(jnp.int32)
        inside = (slot_of >= 0) & (slot_of < plane)
        column = jnp.where(inside, (slot_of * rings + ring_of) * pair_rows + rank_of, -1)
        places = jnp.arange(slots * pair_rows, dtype=jnp.int32)[:, None, None]
        coarse_of = lax.reduce_precision(facts[:, 2], 8, 7)
        fine_of = facts[:, 2] - coarse_of
        ones, coarse, fine = 0.0, 0.0, 0.0
        for k in range(top):
            hit = column[None, :, k] == places
            ones = ones + jnp.where(hit, 1.0, 0.0)
            coarse = coarse + jnp.where(hit, coarse_of[None, :, k], 0.0)
            fine = fine + jnp.where(hit, fine_of[None, :, k], 0.0)
        return [
            w.astype(jnp.bfloat16).reshape(slots * pair_rows, rings * token_count)
            for w in (coarse, fine, ones)
        ]

    def to_plane(rows):
        chunks = rows.reshape(plane, rings * pair_rows, -1)
        return lax.all_to_all(chunks, PLANE, 0, 0, tiled=True).reshape(slots * pair_rows, -1)

    gate_weight, up_weight, down_weight = w_gate[0], w_up[0], w_down[0]
    at = group.astype(jnp.int32).reshape(1)
    inputs, cot_in, gate, up_proj, hidden, send_down = front(at, arrived, gate_weight, up_weight)
    got_down = swap_low(send_down)
    out_rows = to_plane(expert(at, hidden, down_weight))
    d_gate, d_up, send_both = second(at, inputs, cot_in, down_weight, gate, up_proj)
    got_both = swap_low(send_both)
    row_left = row_gradient(at, 0, 5, 256, 0, d_gate, d_up, gate_weight, up_weight)
    tied = lax.optimization_barrier((d_gate, row_left, got_down))
    d_gate, got_down = tied[0], tied[2]
    row_right = row_gradient(at, 5, 3, 256, LONG, d_gate, d_up, gate_weight, up_weight)
    coarse, fine, ones = weights_of(lax.optimization_barrier((*facts, row_right))[:-1])
    left_rows = to_plane(after(row_left, row_right, coarse, fine, ones))
    out_far, out_near = sums(at, out_rows, coarse, fine)
    right_rows = to_plane(after(row_right, out_far))
    kept = keep_half(at, inputs, cot_in, after(hidden, out_far), d_gate, d_up)

    is_anchor = anchors[ep_index] == ep_index
    beside = jnp.minimum(ep_index + 1, ep_count - 1)
    joins = (ep_index + 1 < ep_count) & (anchors[beside] == ep_index)

    def joined(keep, got):
        passed = lax.ppermute(jnp.where(group == 0, got, keep), "core", [(1, 0)]).astype(jnp.float32)
        keep, got = keep.astype(jnp.float32), got.astype(jnp.float32)
        one = jnp.where(group == 0, keep, got)
        two = jnp.where(group == 0, got, keep)
        return one + jnp.where(is_anchor, two, 0.0) + jnp.where(joins, passed, 0.0)

    out_came = swap_high(out_far)
    left_far, left_near = sums(at, after(left_rows, out_far), ones)
    out_near = out_near + after(out_came, left_far).astype(jnp.float32)
    out_others = out_near[token_count:].astype(jnp.bfloat16)
    out_last = swap_low(out_others)
    got_both = after(got_both, left_far, out_others)
    grad_down = joined(kept[0], after(got_down, left_far, out_others))
    left_came = swap_high(left_far)
    right_far, right_near = sums(at, after(right_rows, left_far, got_both, out_others), ones)
    right_came = swap_high(right_far)
    grad_gate = joined(kept[1], got_both[0])
    grad_up = joined(kept[2], got_both[1])
    out_last = after(out_last, right_far)
    mixed = (out_near[:token_count] + out_last.astype(jnp.float32)).astype(jnp.bfloat16)
    left_near = left_near + after(left_came, right_far).astype(jnp.float32)
    left_others = left_near[token_count:].astype(jnp.bfloat16)
    left_last = swap_low(left_others)
    right_came, left_last, grad_down = lax.optimization_barrier((right_came, left_last, grad_down))
    right_near = right_near + right_came.astype(jnp.float32)
    right_last = swap_low(right_near[token_count:].astype(jnp.bfloat16))
    tied = (left_last, right_last, mixed, grad_down, grad_gate, grad_up)
    left_last, right_last, mixed, grad_down, grad_gate, grad_up = lax.optimization_barrier(tied)
    ends = [
        (near[:token_count] + last.astype(jnp.float32)).astype(jnp.bfloat16)
        for near, last in ((left_near, left_last), (right_near, right_last))
    ]
    input_grad = jnp.concatenate(ends, axis=1)
    return (mixed, input_grad, grad_gate[None], grad_up[None], grad_down[None])


def solution(mesh):
    fine = Mesh(mesh.devices.reshape(2, 2, 4, 4, 2), AXES)
    rows = P(AXES, None)
    slot = P(AXES, None, None)
    experts = ("xhi",) + PLANE
    return jax.shard_map(
        on_device,
        mesh=fine,
        in_specs=(rows, rows, rows, rows, P(), slot, slot, slot),
        out_specs=(
            rows,
            rows,
            P(experts, "xlo", None),
            P(experts, "xlo", None),
            P(experts, None, "xlo"),
        ),
        check_vma=False,
    )
```

```python
import functools

import jax
import jax.numpy as jnp
from jax import lax
from jax.experimental import pallas as pl
from jax.experimental.pallas import tpu as pltpu
from jax.sharding import Mesh, PartitionSpec as P

AXES = ("xlo", "xhi", "y", "z", "core")
PLANE = ("y", "z", "core")
LANES = 128
MIB = 1 << 20
LONG = 40_000_000_000


def pack_kernel(pair_rows, route_ref, weight_ref, tok_ref, cot_ref, out_ref, rank_ref, place):
    top, tokens = route_ref.shape
    targets, _, tall, _ = out_ref.shape
    slots = targets * pl.num_programs(0)
    rows = targets * pair_rows
    parts = tall // pair_rows
    step = pl.program_id(0)

    @pl.when(step == 0)
    def _():
        across = lax.broadcasted_iota(jnp.int32, (tokens, tokens), 1)
        down = lax.broadcasted_iota(jnp.int32, (tokens, tokens), 0)
        earlier = (down < across).astype(jnp.bfloat16)
        slot = lax.broadcasted_iota(jnp.int32, (slots, tokens), 0)
        before = jnp.zeros((slots, 1), jnp.float32)
        for k in range(top):
            mine = slot == route_ref[k : k + 1, :]
            marks = mine.astype(jnp.float32)
            ahead = jnp.dot(
                marks.astype(jnp.bfloat16), earlier, preferred_element_type=jnp.float32
            )
            rank = jnp.sum(jnp.where(mine, ahead + before, 0.0), axis=0, keepdims=True)
            before = before + jnp.sum(marks, axis=1, keepdims=True)
            rank_ref[k : k + 1, :] = rank.astype(jnp.int32)
            place[k : k + 1, :] = route_ref[k : k + 1, :] * pair_rows + rank.astype(jnp.int32)

    row = lax.broadcasted_iota(jnp.int32, (rows, tokens), 0) + step * rows
    chosen = jnp.zeros((rows, tokens), jnp.float32)
    weight = jnp.zeros((rows, tokens), jnp.float32)
    for k in range(top):
        hit = row == place[k : k + 1, :]
        chosen = jnp.where(hit, 1.0, chosen)
        weight = jnp.where(hit, weight_ref[k : k + 1, :], weight)
    weight = jnp.sum(weight, axis=1, keepdims=True)
    chosen = chosen.astype(jnp.bfloat16)
    tok = jnp.dot(chosen, tok_ref[...], preferred_element_type=jnp.float32)
    out_ref[:, 0] = tok.reshape(targets, tall, LANES).astype(out_ref.dtype)
    cot = jnp.dot(chosen, cot_ref[...], preferred_element_type=jnp.float32) * weight
    out_ref[:, 1] = cot.reshape(targets, tall, LANES).astype(out_ref.dtype)


def pack(route, weight, tokens, cotangent, slots, pair_rows):
    count, width = tokens.shape
    tall = pair_rows * width // LANES
    block = 32
    whole = lambda i: (0, 0)
    return pl.pallas_call(
        functools.partial(pack_kernel, pair_rows),
        grid=(slots // block,),
        out_shape=(
            pltpu.HBM((slots, 2, tall, LANES), jnp.bfloat16),
            jax.ShapeDtypeStruct(route.shape, jnp.int32),
        ),
        in_specs=[
            pl.BlockSpec(route.shape, whole),
            pl.BlockSpec(weight.shape, whole),
            pl.BlockSpec(tokens.shape, whole),
            pl.BlockSpec(cotangent.shape, whole),
        ],
        out_specs=(
            pl.BlockSpec((block, 2, tall, LANES), lambda i: (i, 0, 0, 0)),
            pl.BlockSpec(route.shape, whole),
        ),
        scratch_shapes=[pltpu.VMEM(route.shape, jnp.int32)],
        compiler_params=pltpu.CompilerParams(vmem_limit_bytes=60 * MIB),
        cost_estimate=cheap(),
    )(route, weight, tokens, cotangent)


def dot(a, b, over_a=1, over_b=0):
    return lax.dot_general(
        a, b, (((over_a,), (over_b,)), ((), ())), preferred_element_type=jnp.float32
    )


def cheap(flops=0):
    return pl.CostEstimate(flops=flops, bytes_accessed=0, transcendentals=0)


def fixed(shape, at=(0, 0)):
    return pl.BlockSpec(shape, lambda n, g: at, pipeline_mode=pl.Buffered(1))


def down(shape):
    return pl.BlockSpec(shape, lambda n, g: (n, 0))


def across(shape):
    return pl.BlockSpec(shape, lambda n, g: (0, n))


def call(kernel, group, steps, ins, outs, *operands, scratch=(), vmem=56 * MIB, cost=0):
    return pl.pallas_call(
        kernel,
        grid_spec=pltpu.PrefetchScalarGridSpec(
            num_scalar_prefetch=1,
            grid=(steps,),
            in_specs=ins,
            out_specs=tuple(spec for spec, _, _ in outs),
            scratch_shapes=list(scratch),
        ),
        out_shape=tuple(pltpu.HBM(shape, kind) for _, shape, kind in outs),
        compiler_params=pltpu.CompilerParams(vmem_limit_bytes=vmem),
        cost_estimate=cheap(cost),
    )(group, *operands)


def front_kernel(
    group,
    arrived,
    gate_in,
    up_in,
    x_out,
    c_out,
    gate_out,
    up_out,
    hidden_out,
    down_out,
    landed,
    gate_w,
    up_w,
    x_all,
    c_all,
    gate_all,
    up_all,
    hidden,
    send_down,
    in_sems,
    w_sems,
    out_sems,
):
    rings, plane, _, tall, _ = arrived.shape
    steps, _, members = landed.shape[:3]
    _, rows, half = x_all.shape
    width = 2 * half
    parts = width // LANES
    inner = hidden.shape[1]
    block = gate_all.shape[2]
    some = rows // steps
    mine = 1 - group[0]
    fetches = [
        pltpu.make_async_copy(
            arrived.at[:, pl.ds(i * members, members)], landed.at[i], in_sems.at[i]
        )
        for i in range(steps)
    ]
    loads = [
        pltpu.make_async_copy(source, target, w_sems.at[i])
        for i, (source, target) in enumerate(
            ((gate_in, gate_w), (up_in, up_w))
        )
    ]
    for copy in fetches + loads:
        copy.start()
    sent = []

    def put(source, target):
        copy = pltpu.make_async_copy(source, target, out_sems.at[len(sent)])
        copy.start()
        sent.append(copy)

    for i in range(steps):
        fetches[i].wait()
        for which, out in enumerate((x_all, c_all)):
            value = landed[i, :, :, which].astype(jnp.float32)
            value = value.reshape(rings, members, tall // parts, parts, LANES)
            value = jnp.swapaxes(value, 0, 1).reshape(some, width).astype(jnp.bfloat16)
            out[0, i * some : (i + 1) * some, :] = value[:, :half]
            out[1, i * some : (i + 1) * some, :] = value[:, half:]
    for copy in loads:
        copy.wait()
    put(x_all, x_out)
    put(c_all, c_out)
    for n in range(inner // block):
        cols = slice(n * block, (n + 1) * block)
        gate = dot(x_all[0], gate_w[:half, cols]) + dot(x_all[1], gate_w[half:, cols])
        up = dot(x_all[0], up_w[:half, cols]) + dot(x_all[1], up_w[half:, cols])
        gate_all[n] = gate
        up_all[n] = up
        put(gate_all.at[n], gate_out.at[n])
        put(up_all.at[n], up_out.at[n])
        hidden[:, cols] = (gate * jax.nn.sigmoid(gate) * up).astype(jnp.bfloat16)
        send_down[cols, :] = dot(hidden[:, cols], c_all[mine], 0, 0).astype(jnp.bfloat16)
        put(send_down.at[cols], down_out.at[cols])
    put(hidden, hidden_out)
    for copy in sent:
        copy.wait()


def front(group, arrived, gate_w, up_w):
    rings, plane, _, tall, _ = arrived.shape
    width, inner = gate_w.shape
    rows = rings * plane * tall * LANES // width
    half, members, block = width // 2, 8, 256
    steps = plane // members
    f32, b16 = jnp.float32, jnp.bfloat16
    shapes = [
        ((2, rows, half), b16),
        ((2, rows, half), b16),
        ((inner // block, rows, block), f32),
        ((inner // block, rows, block), f32),
        ((rows, inner), b16),
        ((inner, half), b16),
    ]
    weights = [((width, inner), b16)] * 2
    sends = 3 + 3 * (inner // block)
    return pl.pallas_call(
        front_kernel,
        out_shape=tuple(pltpu.HBM(*shape) for shape in shapes),
        in_specs=[pl.BlockSpec(memory_space=pltpu.SMEM)]
        + [pl.BlockSpec(memory_space=pl.ANY)] * 3,
        out_specs=tuple(pl.BlockSpec(memory_space=pl.ANY) for _ in shapes),
        scratch_shapes=[pltpu.VMEM((steps, rings, members, 2, tall, LANES), b16)]
        + [pltpu.VMEM(*shape) for shape in weights + shapes]
        + [pltpu.SemaphoreType.DMA((n,)) for n in (steps, len(weights), sends)],
        compiler_params=pltpu.CompilerParams(vmem_limit_bytes=56 * MIB),
        cost_estimate=cheap(),
    )(group, arrived, gate_w, up_w)


def expert_kernel(group, hidden_ref, down_w, out_ref):
    out_ref[...] = dot(hidden_ref[...], down_w[...]).astype(jnp.bfloat16)


def expert(group, hidden, down_w):
    rows, inner = hidden.shape
    width, block = down_w.shape[1], 1024
    return call(
        expert_kernel,
        group,
        width // block,
        [fixed((rows, inner)), across((inner, block))],
        [(across((rows, block)), (rows, width), jnp.bfloat16)],
        hidden,
        down_w,
    )[0]


def second_kernel(group, x_ref, c_ref, down_w, gate_ref, up_ref, dg_ref, du_ref, send_ref, turned):
    @pl.when(pl.program_id(0) == 0)
    def _():
        turned[...] = jnp.transpose(x_ref[0])

    half = x_ref.shape[2]
    back = dot(c_ref[0], down_w[:, :half], 1, 1) + dot(c_ref[1], down_w[:, half:], 1, 1)
    gate, up = gate_ref[0], up_ref[0]
    sigma = jax.nn.sigmoid(gate)
    d_gate = (back * up * sigma * (1.0 + gate * (1.0 - sigma))).astype(jnp.bfloat16)
    d_up = (back * (gate * sigma)).astype(jnp.bfloat16)
    dg_ref[...] = d_gate
    du_ref[...] = d_up
    send_ref[0] = dot(turned[...], d_gate).astype(jnp.bfloat16)
    send_ref[1] = dot(turned[...], d_up).astype(jnp.bfloat16)


def second(group, inputs, cot_in, down_w, gate, up):
    _, rows, half = inputs.shape
    chunks, _, block = gate.shape
    inner, width = chunks * block, 2 * half
    chunk = pl.BlockSpec((1, rows, block), lambda n, g: (n, 0, 0))
    b16 = jnp.bfloat16
    away = pl.BlockSpec((1, rows, half), lambda n, g: (1 - g[0], 0, 0), pipeline_mode=pl.Buffered(1))
    return call(
        second_kernel,
        group,
        inner // block,
        [
            away,
            fixed((2, rows, half), (0, 0, 0)),
            down((block, width)),
            chunk,
            chunk,
        ],
        [
            (across((rows, block)), (rows, inner), b16),
            (across((rows, block)), (rows, inner), b16),
            (pl.BlockSpec((2, half, block), lambda n, g: (0, 0, n)), (2, half, inner), b16),
        ],
        inputs,
        cot_in,
        down_w,
        gate,
        up,
        scratch=[pltpu.VMEM((half, rows), b16)],
    )


def rows_kernel(group, dg_ref, du_ref, gate_w, up_w, out_ref):
    out_ref[...] = (dot(dg_ref[...], gate_w[...], 1, 1) + dot(du_ref[...], up_w[...], 1, 1)).astype(
        jnp.bfloat16
    )


def row_gradient(group, first, steps, block, cost, d_gate, d_up, gate_w, up_w):
    rows, inner = d_gate.shape
    part = pl.BlockSpec((block, inner), lambda n, g: (n + first, 0))
    return call(
        rows_kernel,
        group,
        steps,
        [fixed((rows, inner)), fixed((rows, inner)), part, part],
        [(across((rows, block)), (rows, steps * block), jnp.bfloat16)],
        d_gate,
        d_up,
        gate_w,
        up_w,
        cost=cost,
    )[0]


def keep_kernel(group, x_ref, c_ref, hidden_ref, dg_ref, du_ref, keep_d, keep_g, keep_u):
    keep_d[...] = dot(hidden_ref[...], c_ref[0], 0, 0).astype(jnp.bfloat16)
    turned = jnp.transpose(x_ref[0])
    keep_g[...] = dot(turned, dg_ref[...]).astype(jnp.bfloat16)
    keep_u[...] = dot(turned, du_ref[...]).astype(jnp.bfloat16)


def keep_half(group, inputs, cot_in, hidden, d_gate, d_up):
    _, rows, half = inputs.shape
    inner = hidden.shape[1]
    block = 384
    b16 = jnp.bfloat16
    here = pl.BlockSpec((1, rows, half), lambda n, g: (g[0], 0, 0), pipeline_mode=pl.Buffered(1))
    return call(
        keep_kernel,
        group,
        inner // block,
        [here, here] + [across((rows, block))] * 3,
        [
            (down((block, half)), (inner, half), b16),
            (across((half, block)), (half, inner), b16),
            (across((half, block)), (half, inner), b16),
        ],
        inputs,
        cot_in,
        hidden,
        d_gate,
        d_up,
    )


def sums_kernel(group, *refs):
    *weights, rows_ref, far_ref, near_ref = refs
    total = sum(dot(w[...], rows_ref[...], 0, 0) for w in weights)
    count = far_ref.shape[0]
    far_ref[...] = total[:count].astype(jnp.bfloat16)
    near_ref[...] = total[count:]


def sums(group, rows, *weights):
    count, targets = weights[0].shape
    width = rows.shape[1]
    block = width // 2
    part = targets // 2
    return call(
        sums_kernel,
        group,
        width // block,
        [fixed((count, targets)) for _ in weights] + [across((count, block))],
        [
            (across((part, block)), (part, width), jnp.bfloat16),
            (across((part, block)), (part, width), jnp.float32),
        ],
        *weights,
        rows,
    )


def over(axes, sizes, move):
    pairs = []
    total = 1
    for n in sizes:
        total *= n
    for i in range(total):
        at, rest = [], i
        for n in reversed(sizes):
            at.append(rest % n)
            rest //= n
        to = move(tuple(reversed(at)))
        if to is not None:
            j = 0
            for n, c in zip(sizes, to, strict=True):
                j = j * n + c
            pairs.append((i, j))
    return pairs


def swap_low(block):
    return lax.ppermute(block, "xlo", [(0, 1), (1, 0)])


def swap_high(block):
    route = over(("xlo", "xhi"), (2, 2), lambda c: (1 - c[0], 1 - c[1]))
    return lax.ppermute(block, ("xlo", "xhi"), route)


def after(value, *others):
    return lax.optimization_barrier((value,) + others)[0]


def on_device(tokens, cotangent, combine, route, anchors, w_gate, w_up, w_down):
    token_count, width = tokens.shape
    top = route.shape[1]
    rings = lax.axis_size(("xlo", "xhi"))
    plane = lax.axis_size(PLANE)
    slots = rings * plane
    pair_rows = 3 * token_count * top // (2 * slots)
    half = width // 2
    group = lax.axis_index("xlo")
    high = lax.axis_index("xhi")
    ring_at = lax.axis_index(("xlo", "xhi"))
    ep_index = lax.axis_index(("xhi",) + PLANE)
    ep_count = lax.axis_size(("xhi",) + PLANE)

    weight = jnp.transpose(combine)
    target = jnp.transpose(route)
    packed, rank = pack(target, weight, tokens, cotangent, slots, pair_rows)
    arrived = lax.all_to_all(packed.reshape(slots, -1, LANES), AXES, 0, 0, tiled=True).reshape(
        rings, plane, 2, -1, LANES
    )

    facts = jnp.concatenate([target.astype(jnp.float32), rank.astype(jnp.float32), weight, weight])
    opposite = lax.ppermute(facts, "xhi", [(0, 1), (1, 0)])
    facts = [swap_high(facts), opposite, facts, swap_low(facts)]
    arrived, *facts = lax.optimization_barrier((arrived, *facts))

    def weights_of(facts):
        facts = jnp.stack(facts).reshape(rings, 4, top, token_count)
        ring_of = jnp.stack(
            [
                (1 - group) * 2 + 1 - high,
                group * 2 + 1 - high,
                group * 2 + high,
                (1 - group) * 2 + high,
            ]
        )[:, None, None]
        slot_of = facts[:, 0].astype(jnp.int32) - ring_at * plane
        rank_of = facts[:, 1].astype(jnp.int32)
        inside = (slot_of >= 0) & (slot_of < plane)
        column = jnp.where(inside, (slot_of * rings + ring_of) * pair_rows + rank_of, -1)
        places = jnp.arange(slots * pair_rows, dtype=jnp.int32)[:, None, None]
        coarse_of = lax.reduce_precision(facts[:, 2], 8, 7)
        fine_of = facts[:, 2] - coarse_of
        ones, coarse, fine = 0.0, 0.0, 0.0
        for k in range(top):
            hit = column[None, :, k] == places
            ones = ones + jnp.where(hit, 1.0, 0.0)
            coarse = coarse + jnp.where(hit, coarse_of[None, :, k], 0.0)
            fine = fine + jnp.where(hit, fine_of[None, :, k], 0.0)
        return [
            w.astype(jnp.bfloat16).reshape(slots * pair_rows, rings * token_count)
            for w in (coarse, fine, ones)
        ]

    def to_plane(rows):
        chunks = rows.reshape(plane, rings * pair_rows, -1)
        return lax.all_to_all(chunks, PLANE, 0, 0, tiled=True).reshape(slots * pair_rows, -1)

    gate_weight, up_weight, down_weight = w_gate[0], w_up[0], w_down[0]
    at = group.astype(jnp.int32).reshape(1)
    inputs, cot_in, gate, up_proj, hidden, send_down = front(at, arrived, gate_weight, up_weight)
    got_down = swap_low(send_down)
    out_rows = to_plane(expert(at, hidden, down_weight))
    d_gate, d_up, send_both = second(at, inputs, cot_in, down_weight, gate, up_proj)
    got_both = swap_low(send_both)
    row_left = row_gradient(at, 0, 5, 256, 0, d_gate, d_up, gate_weight, up_weight)
    tied = lax.optimization_barrier((d_gate, row_left, got_down))
    d_gate, got_down = tied[0], tied[2]
    row_right = row_gradient(at, 5, 3, 256, LONG, d_gate, d_up, gate_weight, up_weight)
    coarse, fine, ones = weights_of(lax.optimization_barrier((*facts, row_right))[:-1])
    left_rows = to_plane(after(row_left, row_right, coarse, fine, ones))
    out_far, out_near = sums(at, out_rows, coarse, fine)
    right_rows = to_plane(after(row_right, out_far))
    kept = keep_half(at, inputs, cot_in, after(hidden, out_far), d_gate, d_up)

    is_anchor = anchors[ep_index] == ep_index
    beside = jnp.minimum(ep_index + 1, ep_count - 1)
    joins = (ep_index + 1 < ep_count) & (anchors[beside] == ep_index)

    def joined(keep, got):
        passed = lax.ppermute(jnp.where(group == 0, got, keep), "core", [(1, 0)]).astype(jnp.float32)
        keep, got = keep.astype(jnp.float32), got.astype(jnp.float32)
        one = jnp.where(group == 0, keep, got)
        two = jnp.where(group == 0, got, keep)
        return one + jnp.where(is_anchor, two, 0.0) + jnp.where(joins, passed, 0.0)

    out_came = swap_high(out_far)
    left_far, left_near = sums(at, after(left_rows, out_far), ones)
    out_near = out_near + after(out_came, left_far).astype(jnp.float32)
    out_others = out_near[token_count:].astype(jnp.bfloat16)
    out_last = swap_low(out_others)
    got_both = after(got_both, left_far, out_others)
    grad_down = joined(kept[0], after(got_down, left_far, out_others))
    left_came = swap_high(left_far)
    right_far, right_near = sums(at, after(right_rows, left_far, got_both, out_others), ones)
    right_came = swap_high(right_far)
    grad_gate = joined(kept[1], got_both[0])
    grad_up = joined(kept[2], got_both[1])
    out_last = after(out_last, right_far)
    mixed = (out_near[:token_count] + out_last.astype(jnp.float32)).astype(jnp.bfloat16)
    left_near = left_near + after(left_came, right_far).astype(jnp.float32)
    left_others = left_near[token_count:].astype(jnp.bfloat16)
    left_last = swap_low(left_others)
    right_came, left_last, grad_down = lax.optimization_barrier((right_came, left_last, grad_down))
    right_near = right_near + right_came.astype(jnp.float32)
    right_last = swap_low(right_near[token_count:].astype(jnp.bfloat16))
    tied = (left_last, right_last, mixed, grad_down, grad_gate, grad_up)
    left_last, right_last, mixed, grad_down, grad_gate, grad_up = lax.optimization_barrier(tied)
    ends = [
        (near[:token_count] + last.astype(jnp.float32)).astype(jnp.bfloat16)
        for near, last in ((left_near, left_last), (right_near, right_last))
    ]
    input_grad = jnp.concatenate(ends, axis=1)
    return (mixed, input_grad, grad_gate[None], grad_up[None], grad_down[None])


def solution(mesh):
    fine = Mesh(mesh.devices.reshape(2, 2, 4, 4, 2), AXES)
    rows = P(AXES, None)
    slot = P(AXES, None, None)
    experts = ("xhi",) + PLANE
    return jax.shard_map(
        on_device,
        mesh=fine,
        in_specs=(rows, rows, rows, rows, P(), slot, slot, slot),
        out_specs=(
            rows,
            rows,
            P(experts, "xlo", None),
            P(experts, "xlo", None),
            P(experts, None, "xlo"),
        ),
        check_vma=False,
    )
```
